512 devices in a mesh: seg: 64 (over y, z_lo, core), sec: 8 (over x, z_hi).
Axes of the slice: x: 4, y: 4, z: 16 (z_hi: 2, z_lo: 8; z = z_hi * 8 + z_lo), core: 2. Of those that a mesh axis runs over, the one named last changes fastest.
Arguments:
- psi_start: bfloat16 [64, 8, 512, 512], P('seg', 'sec'), may hold values from -6 to 6
- left_site: bfloat16 [64, 8, 512, 512], P('seg', 'sec'), may hold values from -2 to 2
- left_terms: bfloat16 [64, 8, 3, 512, 512], P('seg', 'sec'), may hold values from -20 to 20
- right_terms: bfloat16 [64, 8, 2, 512, 512], P('seg', 'sec'), may hold values from -1 to 1
- start_cols: bfloat16 [8, 512, 256], P('sec'), may hold values from -6 to 6
- sector_table: int32 [8, 3], P('sec'), may hold values from 128 to 512, as said below
Outputs:
- truncated: bfloat16 [64, 8, 512, 512], P('seg', 'sec')
- density_back: bfloat16 [64, 8, 512, 512], P('seg', 'sec')
The draws below stay inside these ranges and needn't reach their ends.
Inputs may be any that keep to these rules, and one draw needn't show every extreme that they name: `sector_table`: live rows and live columns lie between 256 and 512, kept ranks between 128 and 256; some sector has 512 live rows and columns and rank 256.
All inputs are finite; a program needn't handle non-finite values.
Results may differ from the reference program's by a relative error of at most 0.024.
Values may be sent and summed in bfloat16 or wider, within the bound.
A program may use at most 64 MiB of HBM per device.

```python
import jax
import jax.numpy as jnp
from jax import lax

BLK = 512
RMAX = 256
TERMS = 3
SEGMENTS = 64
SECTORS = 8


def draw_sector_table(key, part):
    key = jax.random.fold_in(key, 7)
    key_rows, key_cols, key_rank, key_pick = jax.random.split(key, 4)
    rows = jax.random.randint(key_rows, (SECTORS,), BLK // 2, BLK + 1)
    cols = jax.random.randint(key_cols, (SECTORS,), BLK // 2, BLK + 1)
    rank = jax.random.randint(key_rank, (SECTORS,), RMAX // 2, RMAX + 1)
    pick = jax.random.randint(key_pick, (), 0, SECTORS)
    chosen = jnp.arange(SECTORS, dtype=jnp.int32) == pick
    rows = jnp.where(chosen, BLK, rows)
    cols = jnp.where(chosen, BLK, cols)
    rank = jnp.where(chosen, RMAX, rank)
    return jnp.stack([rows, cols, rank], axis=1).astype(jnp.int32)


def draw_psi_start(key, part):
    key = jax.random.fold_in(key, 3)
    key_common, key_single = jax.random.split(key, 2)
    outer_shape = (SEGMENTS, 1, BLK, BLK)
    full_shape = (SEGMENTS, SECTORS, BLK, BLK)
    common = jax.random.truncated_normal(key_common, -6.0, 6.0, outer_shape, jnp.float32)
    single = jax.random.truncated_normal(key_single, -6.0, 6.0, full_shape, jnp.float32)
    values = 0.8 * common + 0.6 * single
    return jnp.clip(values, -6.0, 6.0).astype(jnp.bfloat16)


def draw_left_site(key, part):
    key = jax.random.fold_in(key, 5)
    key_common, key_single = jax.random.split(key, 2)
    outer_shape = (SEGMENTS, 1, BLK, BLK)
    full_shape = (SEGMENTS, SECTORS, BLK, BLK)
    common = jax.random.truncated_normal(key_common, -6.0, 6.0, outer_shape, jnp.float32)
    single = jax.random.truncated_normal(key_single, -6.0, 6.0, full_shape, jnp.float32)
    values = 0.8 * common + 0.6 * single
    return (values / jnp.sqrt(jnp.float32(BLK))).astype(jnp.bfloat16)


def draw_left_terms(key, part):
    key = jax.random.fold_in(key, 11)
    key_common, key_single = jax.random.split(key, 2)
    outer_shape = (SEGMENTS, 1, TERMS, BLK, BLK)
    full_shape = (SEGMENTS, SECTORS, TERMS, BLK, BLK)
    common = jax.random.truncated_normal(key_common, -6.0, 6.0, outer_shape, jnp.float32)
    single = jax.random.truncated_normal(key_single, -6.0, 6.0, full_shape, jnp.float32)
    noise = 0.8 * common + 0.6 * single
    rise = 3.0
    hopping = 8.0
    noise = noise / jnp.sqrt(jnp.float32(BLK))
    level = jnp.arange(SECTORS, dtype=jnp.float32) / max(SECTORS - 1, 1)
    strength = 2.0 * jnp.power(rise, level)
    first_term = (jnp.arange(TERMS, dtype=jnp.int32) == 0).astype(jnp.float32)
    scales = strength[:, None] * first_term[None, :] + hopping * (1.0 - first_term[None, :])
    identity = jnp.eye(BLK, dtype=jnp.float32)
    diagonal = scales[:, :, None, None] * identity[None, None]
    return (noise + diagonal[None]).astype(jnp.bfloat16)


def draw_right_terms(key, part):
    key = jax.random.fold_in(key, 13)
    full_shape = (SEGMENTS, SECTORS, 2, BLK, BLK)
    noise = jax.random.truncated_normal(key, -6.0, 6.0, full_shape, jnp.float32)
    noise = 0.25 * noise / jnp.sqrt(jnp.float32(BLK))
    identity = jnp.eye(BLK, dtype=jnp.float32)
    return (noise + 0.5 * identity[None, None, None]).astype(jnp.bfloat16)


def levels(key, dims, cuts, least, high):
    def one(position, blocks):
        steps = jax.random.uniform(jax.random.fold_in(jax.random.fold_in(key, 6), position), (blocks,), jnp.float32, least / len(cuts), high / len(cuts))
        return jnp.repeat(jnp.exp(steps), dims[position] // blocks).reshape((-1,) + (1,) * (len(dims) - position - 1))

    level = one(*cuts[0])
    for cut in cuts[1:]:
        level = level * one(*cut)
    return level


def scatter_about(key, extent, spread, bound, shards=(), kind=jnp.bfloat16):
    entries = spread * jax.random.normal(key, extent, jnp.float32)
    if shards:
        entries = entries * levels(key, extent, shards, -0.22, 0.18)
    return jnp.clip(entries, -bound, bound).astype(kind)


def setup_inputs(seed: int = 0) -> dict:
    seeds = jax.random.split(jax.random.key(seed), 7)
    psi_start = draw_psi_start(jax.random.fold_in(seeds[6], 71), 0)
    left_site = draw_left_site(jax.random.fold_in(seeds[6], 71), 0)
    left_terms = draw_left_terms(jax.random.fold_in(seeds[6], 71), 0)
    right_terms = draw_right_terms(jax.random.fold_in(seeds[6], 71), 0)
    start_cols = scatter_about(seeds[4], (SECTORS, BLK, RMAX), 1.0, 6.0, ((0, 8),))
    sector_table = draw_sector_table(jax.random.fold_in(seeds[6], 71), 0)
    return dict(psi_start=psi_start, left_site=left_site, left_terms=left_terms, right_terms=right_terms, start_cols=start_cols, sector_table=sector_table)


eps = 1e-06

def build_left(site, terms):
    part = jnp.einsum('skij,sjl->skil', terms.astype(jnp.float32), site.astype(jnp.float32)).astype(jnp.bfloat16)
    return jnp.einsum('sji,skjl->skil', site.astype(jnp.float32), part.astype(jnp.float32)).astype(jnp.bfloat16)

def masks(table):
    index = jnp.arange(BLK, dtype=jnp.int32)
    mask = ((index[None, :, None] < table[:, 0][:, None, None]) & (index[None, None, :] < table[:, 1][:, None, None])).astype(jnp.float32)
    keep = (jnp.arange(RMAX, dtype=jnp.int32)[None, :] < table[:, 2][:, None]).astype(jnp.float32)
    return (mask, keep)

def mult(left, right):
    return jnp.einsum('sij,sjk->sik', left.astype(jnp.float32), right.astype(jnp.float32))

def hamil(vec, env, right, mask):
    zero = jnp.zeros((1, BLK, BLK), jnp.bfloat16)
    below = jnp.concatenate([zero, vec[:-1]], axis=0)
    above = jnp.concatenate([vec[1:], zero], axis=0)
    lower = mult(below, right[:, 0]).astype(jnp.bfloat16)
    upper = mult(above, right[:, 1]).astype(jnp.bfloat16)
    total = mult(env[:, 0], vec) + mult(env[:, 1], lower) + mult(env[:, 2], upper)
    return total * mask

def merge_one(psi, env, right, cols, table):
    mask, keep = masks(table)
    start = psi.astype(jnp.float32) * mask
    first = (start / jnp.sqrt(jnp.sum(start * start) + eps)).astype(jnp.bfloat16)
    firstf = first.astype(jnp.float32)
    image = hamil(first, env, right, mask)
    alpha = jnp.sum(firstf * image)
    resid = image - alpha * firstf
    beta = jnp.sqrt(jnp.sum(resid * resid) + eps)
    second = (resid / beta).astype(jnp.bfloat16)
    secondf = second.astype(jnp.float32)
    gamma = jnp.sum(secondf * hamil(second, env, right, mask))
    lowest = 0.5 * (alpha + gamma) - jnp.sqrt(0.25 * (alpha - gamma) ** 2 + beta ** 2)
    united = (gamma - lowest) * firstf - beta * secondf
    factor = jnp.sqrt(jnp.float32(SECTORS * BLK * BLK)) / jnp.sqrt(jnp.sum(united * united) + eps)
    ground = (united * factor).astype(jnp.bfloat16)
    ranged = (mult(ground, cols) * keep[:, None, :]).astype(jnp.bfloat16)
    rangef = ranged.astype(jnp.float32)
    gram = jnp.einsum('sir,sit->srt', rangef, rangef) + jnp.eye(RMAX, dtype=jnp.float32)[None] * (1.0 - keep)[:, None, :]
    factors = jnp.linalg.cholesky(gram)
    solved = jax.vmap(lambda low, rhs: jax.scipy.linalg.solve_triangular(low, rhs, lower=True))(factors, jnp.swapaxes(rangef, 1, 2))
    basis = jnp.swapaxes(solved, 1, 2).astype(jnp.bfloat16)
    coeff = jnp.einsum('sir,sij->srj', basis.astype(jnp.float32), ground.astype(jnp.float32)).astype(jnp.bfloat16)
    kept = mult(basis, coeff).astype(jnp.bfloat16)
    keptf = kept.astype(jnp.float32)
    dens = (jnp.einsum('sij,skj->sik', keptf, keptf) / BLK).astype(jnp.bfloat16)
    return (kept, dens)

def reference(psi_start, left_site, left_terms, right_terms, start_cols, sector_table):
    built = lax.map(lambda pair: build_left(pair[0], pair[1]), (left_site, left_terms))
    env = jnp.concatenate([jnp.zeros_like(built[:1]), built[:-1]], axis=0)
    kept, dens = lax.map(lambda trio: merge_one(trio[0], trio[1], trio[2], start_cols, sector_table), (psi_start, env, right_terms))
    back = jnp.concatenate([dens[1:], jnp.zeros_like(dens[:1])], axis=0)
    return (kept, back)
```

```python
import functools
import math

import jax
import jax.numpy as jnp
from jax import lax
from jax.experimental import pallas as pl
from jax.experimental.pallas import tpu as pltpu
from jax.sharding import PartitionSpec as P

eps = 1e-06
MESH = pl.DeviceIdType.MESH
CHUNKS = 8


def dot(left, right):
    return jnp.dot(left, right, preferred_element_type=jnp.float32)


def dot_t(left, right):
    return lax.dot_general(
        left, right, (((0,), (0,)), ((), ())), preferred_element_type=jnp.float32
    )


def total(block):
    return jnp.sum(jnp.sum(block, axis=0, keepdims=True), axis=1, keepdims=True)


def pack(values):
    row = lax.broadcasted_iota(jnp.int32, (8, 128), 0)
    tile = jnp.zeros((8, 128), jnp.float32)
    for k, value in enumerate(values):
        tile = jnp.where(row == k, value, tile)
    return tile


def lanczos_kernel(
    table_ref, psi_ref, site_ref, terms_ref, right_ref, ground_ref,
    start, start_z, start_x, site_t, part, built, env, vec, vec_z, vec_x,
    low_z, low_x, image, resid, resid_z, resid_x, adj_z, adj_x,
    sums1, sums2, sums3,
    z_send, z_recv, x_send, x_recv, env_send, env_recv, sum_send, sum_recv,
):
    seg, sec = lax.axis_index("seg"), lax.axis_index("sec")
    segs, secs = lax.axis_size("seg"), lax.axis_size("sec")
    width = psi_ref.shape[0]
    rows = width // CHUNKS
    half = width // 2
    parity = lax.rem(sec, 2)
    partner = sec + 1 - 2 * parity
    relay = lax.rem(sec + 2 - 4 * parity + secs, secs)
    origin = lax.rem(sec + 2 * parity - 1 + secs, secs)
    nxt, prv = lax.rem(seg + 1, segs), lax.rem(seg + segs - 1, segs)
    peers = [(seg, lax.rem(sec + d, secs)) for d in range(1, secs)]

    barrier = pltpu.get_barrier_semaphore()
    neighbours = peers + [(nxt, sec), (prv, sec)]
    for device in neighbours:
        pl.semaphore_signal(barrier, inc=1, device_id=device, device_id_type=MESH)
    pl.semaphore_wait(barrier, len(neighbours))

    def chunk(i):
        return pl.ds(pl.multiple_of(i * rows, rows), rows)

    def z_copy(phase, i, source, target):
        return pltpu.make_async_remote_copy(
            source.at[chunk(i)], target.at[chunk(i)],
            z_send.at[phase, i], z_recv.at[phase, i],
            device_id=(seg, partner), device_id_type=MESH,
        )

    def x_copy(phase, i, source, target):
        return pltpu.make_async_remote_copy(
            source.at[chunk(i)], target.at[chunk(i)],
            x_send.at[phase, i], x_recv.at[phase, i],
            device_id=(seg, relay), device_id_type=MESH,
        )

    def env_copy(k):
        return pltpu.make_async_remote_copy(
            built.at[k], env.at[k], env_send.at[k], env_recv.at[k],
            device_id=(nxt, sec), device_id_type=MESH,
        )

    def sum_copies(phase, buffer):
        return [
            pltpu.make_async_remote_copy(
                buffer.at[sec], buffer.at[sec],
                sum_send.at[phase, d], sum_recv.at[phase, d],
                device_id=peers[d], device_id_type=MESH,
            )
            for d in range(secs - 1)
        ]

    def share(phase, buffer, values):
        buffer[sec] = pack(values)
        for copy in sum_copies(phase, buffer):
            copy.start()

    def collect(phase, buffer):
        for copy in sum_copies(phase, buffer):
            copy.wait()

    def entry(buffer, s, k):
        return buffer[s, pl.ds(k, 1), pl.ds(0, 1)]

    def summed(buffer, k):
        value = entry(buffer, 0, k)
        for s in range(1, secs):
            value = value + entry(buffer, s, k)
        return value

    live_rows, live_cols = table_ref[0, 0], table_ref[0, 1]

    def mask(first, count):
        i = lax.broadcasted_iota(jnp.int32, (count, width), 0) + first
        j = lax.broadcasted_iota(jnp.int32, (count, width), 1)
        return (i < live_rows) & (j < live_cols)

    zero = jnp.zeros((1, 1), jnp.float32)

    def begin(i, norm):
        piece = jnp.where(mask(i * rows, rows), psi_ref[chunk(i)].astype(jnp.float32), 0.0)
        start[chunk(i)] = piece.astype(jnp.bfloat16)
        z_copy(0, i, start, start_z).start()
        return norm + total(piece * piece)

    norm = lax.fori_loop(0, CHUNKS, begin, zero)
    share(0, sums1, [norm])

    site_t[...] = site_ref[...].T

    def build(k, _):
        def left(b, _):
            block = pl.ds(pl.multiple_of(b * half, half), half)
            part[block] = dot(terms_ref[k, block], site_ref[...]).astype(jnp.bfloat16)
            return 0

        lax.fori_loop(0, 2, left, 0)

        def right(b, _):
            block = pl.ds(pl.multiple_of(b * half, half), half)
            built[k, block] = dot(site_t[block], part[...]).astype(jnp.bfloat16)
            return 0

        lax.fori_loop(0, 2, right, 0)
        env_copy(k).start()
        return 0

    lax.fori_loop(0, 3, build, 0)

    collect(0, sums1)
    scale = 1.0 / jnp.sqrt(summed(sums1, 0) + eps)
    has_env = jnp.where(seg > 0, 1.0, 0.0).astype(jnp.float32)
    has_x = jnp.where((sec > 0) & (sec < secs - 1), 1.0, 0.0).astype(jnp.float32)

    def scaled(i, source, target):
        piece = (source[chunk(i)].astype(jnp.float32) * scale).astype(jnp.bfloat16)
        target[chunk(i)] = piece
        return piece

    def own(i, _):
        scaled(i, start, vec)
        return 0

    lax.fori_loop(0, CHUNKS, own, 0)

    right_z, right_x = right_ref.at[1 - parity], right_ref.at[parity]
    env_z, env_x = env.at[2 - parity], env.at[1 + parity]

    def relay_z(phase, i, source, target_z, target_x):
        z_copy(phase, i, source, target_z).wait_recv()
        x_copy(phase, i, target_z, target_x).start()

    def first_z(i):
        low_z[chunk(i)] = dot(scaled(i, start_z, vec_z), right_z[...]).astype(jnp.bfloat16)

    def first_x(i):
        x_copy(0, i, start_z, start_x).wait_recv()
        low_x[chunk(i)] = (dot(scaled(i, start_x, vec_x), right_x[...]) * has_x).astype(jnp.bfloat16)

    relay_z(0, 0, start, start_z, start_x)
    first_z(0)

    def arrive(i, _):
        relay_z(0, i, start, start_z, start_x)
        first_z(i)
        first_x(i - 1)
        return 0

    lax.fori_loop(1, CHUNKS, arrive, 0)
    first_x(CHUNKS - 1)
    for k in range(3):
        env_copy(k).wait_recv()

    def apply(b, sums):
        block = pl.ds(pl.multiple_of(b * half, half), half)
        value = dot(env[0, block], vec[...])
        value += dot(env_z[block], low_z[...])
        value += dot(env_x[block], low_x[...])
        value = jnp.where(mask(b * half, half), value * has_env, 0.0)
        image[block] = value
        mine = vec[block].astype(jnp.float32)
        return sums[0] + total(mine * value), sums[1] + total(mine * mine)

    along, size = lax.fori_loop(0, 2, apply, (zero, zero))
    ratio = jnp.where(size > 0.0, along / jnp.where(size > 0.0, size, 1.0), 0.0)

    def reduce(i, sums):
        mine = vec[chunk(i)].astype(jnp.float32)
        piece = image[chunk(i)] - ratio * mine
        image[chunk(i)] = piece
        resid[chunk(i)] = piece.astype(jnp.bfloat16)
        z_copy(1, i, resid, resid_z).start()
        return sums[0] + total(piece * piece), sums[1] + total(mine * piece)

    rho, cross = lax.fori_loop(0, CHUNKS, reduce, (zero, zero))
    share(1, sums2, [along, size, rho, cross, ratio])
    collect(1, sums2)
    alpha = summed(sums2, 0)
    beta_sq = zero
    for s in range(secs):
        delta = entry(sums2, s, 4) - alpha
        beta_sq = beta_sq + entry(sums2, s, 2) + 2.0 * delta * entry(sums2, s, 3)
        beta_sq = beta_sq + delta * delta * entry(sums2, s, 1)
    beta = jnp.sqrt(jnp.maximum(beta_sq, 0.0) + eps)
    inverse = 1.0 / beta
    shift_own = ratio - alpha
    shift_z = entry(sums2, partner, 4) - alpha
    shift_x = entry(sums2, origin, 4) - alpha

    def second(i, sums):
        mine = vec[chunk(i)].astype(jnp.float32)
        piece = ((image[chunk(i)] + shift_own * mine) * inverse).astype(jnp.bfloat16)
        start[chunk(i)] = piece
        wide = piece.astype(jnp.float32)
        return sums[0] + total(mine * wide), sums[1] + total(wide * wide)

    for i in range(CHUNKS):
        z_copy(0, i, start, start_z).wait_send()
    overlap, size2 = lax.fori_loop(0, CHUNKS, second, (zero, zero))

    def adjoint(b, gamma):
        block = pl.ds(pl.multiple_of(b * half, half), half)
        adj_z[block] = dot_t(env_z[:, block], start[...])
        adj_x[block] = dot_t(env_x[:, block], start[...])
        return gamma + total(start[block].astype(jnp.float32) * dot(env[0, block], start[...]))

    gamma = zero
    for b in range(2):
        gamma = adjoint(b, gamma)

    def second_term(i, source, base, shift, matrix, adj):
        piece = source[chunk(i)].astype(jnp.float32) + shift * base[chunk(i)].astype(jnp.float32)
        piece = (piece * inverse).astype(jnp.bfloat16)
        low = dot(piece, matrix[...]).astype(jnp.bfloat16).astype(jnp.float32)
        return total(low * adj[chunk(i)])

    def second_z(i):
        return second_term(i, resid_z, vec_z, shift_z, right_z, adj_z)

    def second_x(i):
        x_copy(1, i, resid_z, resid_x).wait_recv()
        return second_term(i, resid_x, vec_x, shift_x, right_x, adj_x) * has_x

    relay_z(1, 0, resid, resid_z, resid_x)
    gamma = gamma + second_z(0)

    def arrive2(i, gamma):
        relay_z(1, i, resid, resid_z, resid_x)
        return gamma + second_z(i) + second_x(i - 1)

    gamma = lax.fori_loop(1, CHUNKS, arrive2, gamma)
    gamma = (gamma + second_x(CHUNKS - 1)) * has_env

    share(2, sums3, [gamma, size, overlap, size2])
    collect(2, sums3)
    gamma = summed(sums3, 0)
    lowest = 0.5 * (alpha + gamma) - jnp.sqrt(0.25 * (alpha - gamma) ** 2 + beta**2)
    first = gamma - lowest
    united_sq = (
        first * first * summed(sums3, 1)
        - 2.0 * first * beta * summed(sums3, 2)
        + beta * beta * summed(sums3, 3)
    )
    factor = math.sqrt(secs * width * width) / jnp.sqrt(jnp.maximum(united_sq, 0.0) + eps)

    def finish(i, _):
        united = first * vec[chunk(i)].astype(jnp.float32) - beta * start[chunk(i)].astype(jnp.float32)
        ground_ref[chunk(i)] = (united * factor).astype(jnp.bfloat16)
        return 0

    lax.fori_loop(0, CHUNKS, finish, 0)

    for i in range(CHUNKS):
        x_copy(0, i, start_z, start_x).wait_send()
        x_copy(1, i, resid_z, resid_x).wait_send()
        z_copy(1, i, resid, resid_z).wait_send()
    for k in range(3):
        env_copy(k).wait_send()


def lanczos(table, psi, site, terms, right, secs):
    width = psi.shape[0]
    square = (width, width)
    bf = functools.partial(pltpu.VMEM, dtype=jnp.bfloat16)
    blocks = lambda *lead: pltpu.VMEM((*lead, *square), jnp.bfloat16)
    wide = pltpu.VMEM(square, jnp.float32)
    sums = pltpu.VMEM((secs, 8, 128), jnp.float32)
    dma = pltpu.SemaphoreType.DMA
    vmem = pl.BlockSpec(memory_space=pltpu.VMEM)
    return pl.pallas_call(
        lanczos_kernel,
        out_shape=jax.ShapeDtypeStruct(square, jnp.bfloat16),
        in_specs=[pl.BlockSpec(memory_space=pltpu.SMEM)] + [vmem] * 4,
        out_specs=vmem,
        scratch_shapes=[
            blocks(), blocks(), blocks(), blocks(), blocks(), blocks(3), blocks(3),
            blocks(), blocks(), blocks(), blocks(), blocks(), wide,
            blocks(), blocks(), blocks(), wide, wide,
            sums, sums, sums,
            dma((2, CHUNKS)), dma((2, CHUNKS)), dma((2, CHUNKS)), dma((2, CHUNKS)),
            dma((3,)), dma((3,)), dma((3, secs)), dma((3, secs)),
        ],
        compiler_params=pltpu.CompilerParams(
            collective_id=1, has_side_effects=True, vmem_limit_bytes=40 * 2**20
        ),
        cost_estimate=pl.CostEstimate(flops=16 * 2 * width**3, bytes_accessed=8 * width**2, transcendentals=0),
    )(table, psi, site, terms, right)


def product(left, right):
    return jnp.dot(left, right, preferred_element_type=jnp.float32)


def per_device(psi_start, left_site, left_terms, right_terms, start_cols, sector_table):
    cols = start_cols[0]
    table = sector_table[0]
    width = psi_start.shape[-1]
    kept_cols = cols.shape[1]
    keep = (jnp.arange(kept_cols, dtype=jnp.int32) < table[2]).astype(jnp.float32)
    ground = lanczos(
        sector_table, psi_start[0, 0], left_site[0, 0], left_terms[0, 0], right_terms[0, 0],
        lax.axis_size("sec"),
    )
    ranged = (product(ground, cols) * keep[None, :]).astype(jnp.bfloat16)
    rangef = ranged.astype(jnp.float32)
    gram = product(ranged.T, ranged) + jnp.eye(kept_cols, dtype=jnp.float32) * (1.0 - keep)[None, :]
    factors = jnp.linalg.cholesky(gram)
    solved = jax.scipy.linalg.solve_triangular(factors, rangef.T, lower=True)
    basis = solved.T.astype(jnp.bfloat16)
    coeff = product(basis.T, ground).astype(jnp.bfloat16)
    kept = product(basis, coeff).astype(jnp.bfloat16)
    dens = (product(kept, kept.T) / width).astype(jnp.bfloat16)
    segs = lax.axis_size("seg")
    back = lax.ppermute(dens, "seg", [(i + 1, i) for i in range(segs - 1)])
    return (kept[None, None], back[None, None])


def solution(mesh):
    placed = (
        P("seg", "sec", None, None),
        P("seg", "sec", None, None),
        P("seg", "sec", None, None, None),
        P("seg", "sec", None, None, None),
        P("sec", None, None),
        P("sec", None),
    )
    return jax.shard_map(
        per_device,
        mesh=mesh,
        in_specs=placed,
        out_specs=(P("seg", "sec", None, None), P("seg", "sec", None, None)),
        check_vma=False,
    )
```

```python
import functools
import math

import jax
import jax.numpy as jnp
from jax import lax
from jax.experimental import pallas as pl
from jax.experimental.pallas import tpu as pltpu
from jax.sharding import PartitionSpec as P

eps = 1e-06
MESH = pl.DeviceIdType.MESH
CHUNKS = 8


def dot(left, right):
    return jnp.dot(left, right, preferred_element_type=jnp.float32)


def dot_t(left, right):
    return lax.dot_general(
        left, right, (((0,), (0,)), ((), ())), preferred_element_type=jnp.float32
    )


def total(block):
    return jnp.sum(jnp.sum(block, axis=0, keepdims=True), axis=1, keepdims=True)


def pack(values):
    row = lax.broadcasted_iota(jnp.int32, (8, 128), 0)
    tile = jnp.zeros((8, 128), jnp.float32)
    for k, value in enumerate(values):
        tile = jnp.where(row == k, value, tile)
    return tile


def lanczos_kernel(
    table_ref, psi_ref, site_ref, terms_ref, right_ref, ground_ref,
    start, start_z, start_x, site_t, part, built, env, vec, vec_z, vec_x,
    low_z, low_x, image, resid, resid_z, resid_x, adj_z, adj_x,
    sums1, sums2, sums3,
    z_send, z_recv, x_send, x_recv, env_send, env_recv, sum_send, sum_recv,
):
    seg, sec = lax.axis_index("seg"), lax.axis_index("sec")
    segs, secs = lax.axis_size("seg"), lax.axis_size("sec")
    width = psi_ref.shape[0]
    rows = width // CHUNKS
    half = width // 2
    parity = lax.rem(sec, 2)
    partner = sec + 1 - 2 * parity
    relay = lax.rem(sec + 2 - 4 * parity + secs, secs)
    origin = lax.rem(sec + 2 * parity - 1 + secs, secs)
    nxt, prv = lax.rem(seg + 1, segs), lax.rem(seg + segs - 1, segs)
    peers = [(seg, lax.rem(sec + d, secs)) for d in range(1, secs)]

    barrier = pltpu.get_barrier_semaphore()
    neighbours = peers + [(nxt, sec), (prv, sec)]
    for device in neighbours:
        pl.semaphore_signal(barrier, inc=1, device_id=device, device_id_type=MESH)
    pl.semaphore_wait(barrier, len(neighbours))

    def chunk(i):
        return pl.ds(pl.multiple_of(i * rows, rows), rows)

    def z_copy(phase, i, source, target):
        return pltpu.make_async_remote_copy(
            source.at[chunk(i)], target.at[chunk(i)],
            z_send.at[phase, i], z_recv.at[phase, i],
            device_id=(seg, partner), device_id_type=MESH,
        )

    def x_copy(phase, i, source, target):
        return pltpu.make_async_remote_copy(
            source.at[chunk(i)], target.at[chunk(i)],
            x_send.at[phase, i], x_recv.at[phase, i],
            device_id=(seg, relay), device_id_type=MESH,
        )

    def env_copy(k):
        return pltpu.make_async_remote_copy(
            built.at[k], env.at[k], env_send.at[k], env_recv.at[k],
            device_id=(nxt, sec), device_id_type=MESH,
        )

    def sum_copies(phase, buffer):
        return [
            pltpu.make_async_remote_copy(
                buffer.at[sec], buffer.at[sec],
                sum_send.at[phase, d], sum_recv.at[phase, d],
                device_id=peers[d], device_id_type=MESH,
            )
            for d in range(secs - 1)
        ]

    def share(phase, buffer, values):
        buffer[sec] = pack(values)
        for copy in sum_copies(phase, buffer):
            copy.start()

    def collect(phase, buffer):
        for copy in sum_copies(phase, buffer):
            copy.wait()

    def entry(buffer, s, k):
        return buffer[s, pl.ds(k, 1), pl.ds(0, 1)]

    def summed(buffer, k):
        value = entry(buffer, 0, k)
        for s in range(1, secs):
            value = value + entry(buffer, s, k)
        return value

    live_rows, live_cols = table_ref[0, 0], table_ref[0, 1]

    def mask(first, count):
        i = lax.broadcasted_iota(jnp.int32, (count, width), 0) + first
        j = lax.broadcasted_iota(jnp.int32, (count, width), 1)
        return (i < live_rows) & (j < live_cols)

    zero = jnp.zeros((1, 1), jnp.float32)

    def begin(i, norm):
        piece = jnp.where(mask(i * rows, rows), psi_ref[chunk(i)].astype(jnp.float32), 0.0)
        start[chunk(i)] = piece.astype(jnp.bfloat16)
        z_copy(0, i, start, start_z).start()
        return norm + total(piece * piece)

    norm = lax.fori_loop(0, CHUNKS, begin, zero)
    share(0, sums1, [norm])

    site_t[...] = site_ref[...].T

    def build(k, _):
        def left(b, _):
            block = pl.ds(pl.multiple_of(b * half, half), half)
            part[block] = dot(terms_ref[k, block], site_ref[...]).astype(jnp.bfloat16)
            return 0

        lax.fori_loop(0, 2, left, 0)

        def right(b, _):
            block = pl.ds(pl.multiple_of(b * half, half), half)
            built[k, block] = dot(site_t[block], part[...]).astype(jnp.bfloat16)
            return 0

        lax.fori_loop(0, 2, right, 0)
        env_copy(k).start()
        return 0

    lax.fori_loop(0, 3, build, 0)

    collect(0, sums1)
    scale = 1.0 / jnp.sqrt(summed(sums1, 0) + eps)
    has_env = jnp.where(seg > 0, 1.0, 0.0).astype(jnp.float32)
    has_x = jnp.where((sec > 0) & (sec < secs - 1), 1.0, 0.0).astype(jnp.float32)

    def scaled(i, source, target):
        piece = (source[chunk(i)].astype(jnp.float32) * scale).astype(jnp.bfloat16)
        target[chunk(i)] = piece
        return piece

    def own(i, _):
        scaled(i, start, vec)
        return 0

    lax.fori_loop(0, CHUNKS, own, 0)

    right_z, right_x = right_ref.at[1 - parity], right_ref.at[parity]
    env_z, env_x = env.at[2 - parity], env.at[1 + parity]

    def relay_z(phase, i, source, target_z, target_x):
        z_copy(phase, i, source, target_z).wait_recv()
        x_copy(phase, i, target_z, target_x).start()

    def first_z(i):
        low_z[chunk(i)] = dot(scaled(i, start_z, vec_z), right_z[...]).astype(jnp.bfloat16)

    def first_x(i):
        x_copy(0, i, start_z, start_x).wait_recv()
        low_x[chunk(i)] = (dot(scaled(i, start_x, vec_x), right_x[...]) * has_x).astype(jnp.bfloat16)

    relay_z(0, 0, start, start_z, start_x)
    first_z(0)

    def arrive(i, _):
        relay_z(0, i, start, start_z, start_x)
        first_z(i)
        first_x(i - 1)
        return 0

    lax.fori_loop(1, CHUNKS, arrive, 0)
    first_x(CHUNKS - 1)
    for k in range(3):
        env_copy(k).wait_recv()

    def apply(b, sums):
        block = pl.ds(pl.multiple_of(b * half, half), half)
        value = dot(env[0, block], vec[...])
        value += dot(env_z[block], low_z[...])
        value += dot(env_x[block], low_x[...])
        value = jnp.where(mask(b * half, half), value * has_env, 0.0)
        image[block] = value
        mine = vec[block].astype(jnp.float32)
        return sums[0] + total(mine * value), sums[1] + total(mine * mine)

    along, size = lax.fori_loop(0, 2, apply, (zero, zero))
    ratio = jnp.where(size > 0.0, along / jnp.where(size > 0.0, size, 1.0), 0.0)

    def reduce(i, sums):
        mine = vec[chunk(i)].astype(jnp.float32)
        piece = image[chunk(i)] - ratio * mine
        image[chunk(i)] = piece
        resid[chunk(i)] = piece.astype(jnp.bfloat16)
        z_copy(1, i, resid, resid_z).start()
        return sums[0] + total(piece * piece), sums[1] + total(mine * piece)

    rho, cross = lax.fori_loop(0, CHUNKS, reduce, (zero, zero))
    share(1, sums2, [along, size, rho, cross, ratio])
    collect(1, sums2)
    alpha = summed(sums2, 0)
    beta_sq = zero
    for s in range(secs):
        delta = entry(sums2, s, 4) - alpha
        beta_sq = beta_sq + entry(sums2, s, 2) + 2.0 * delta * entry(sums2, s, 3)
        beta_sq = beta_sq + delta * delta * entry(sums2, s, 1)
    beta = jnp.sqrt(jnp.maximum(beta_sq, 0.0) + eps)
    inverse = 1.0 / beta
    shift_own = ratio - alpha
    shift_z = entry(sums2, partner, 4) - alpha
    shift_x = entry(sums2, origin, 4) - alpha

    def second(i, sums):
        mine = vec[chunk(i)].astype(jnp.float32)
        piece = ((image[chunk(i)] + shift_own * mine) * inverse).astype(jnp.bfloat16)
        start[chunk(i)] = piece
        wide = piece.astype(jnp.float32)
        return sums[0] + total(mine * wide), sums[1] + total(wide * wide)

    for i in range(CHUNKS):
        z_copy(0, i, start, start_z).wait_send()
    overlap, size2 = lax.fori_loop(0, CHUNKS, second, (zero, zero))

    def adjoint(b, gamma):
        block = pl.ds(pl.multiple_of(b * half, half), half)
        adj_z[block] = dot_t(env_z[:, block], start[...])
        adj_x[block] = dot_t(env_x[:, block], start[...])
        return gamma + total(start[block].astype(jnp.float32) * dot(env[0, block], start[...]))

    gamma = zero
    for b in range(2):
        gamma = adjoint(b, gamma)

    def second_term(i, source, base, shift, matrix, adj):
        piece = source[chunk(i)].astype(jnp.float32) + shift * base[chunk(i)].astype(jnp.float32)
        piece = (piece * inverse).astype(jnp.bfloat16)
        low = dot(piece, matrix[...]).astype(jnp.bfloat16).astype(jnp.float32)
        return total(low * adj[chunk(i)])

    def second_z(i):
        return second_term(i, resid_z, vec_z, shift_z, right_z, adj_z)

    def second_x(i):
        x_copy(1, i, resid_z, resid_x).wait_recv()
        return second_term(i, resid_x, vec_x, shift_x, right_x, adj_x) * has_x

    relay_z(1, 0, resid, resid_z, resid_x)
    gamma = gamma + second_z(0)

    def arrive2(i, gamma):
        relay_z(1, i, resid, resid_z, resid_x)
        return gamma + second_z(i) + second_x(i - 1)

    gamma = lax.fori_loop(1, CHUNKS, arrive2, gamma)
    gamma = (gamma + second_x(CHUNKS - 1)) * has_env

    share(2, sums3, [gamma, size, overlap, size2])
    collect(2, sums3)
    gamma = summed(sums3, 0)
    lowest = 0.5 * (alpha + gamma) - jnp.sqrt(0.25 * (alpha - gamma) ** 2 + beta**2)
    first = gamma - lowest
    united_sq = (
        first * first * summed(sums3, 1)
        - 2.0 * first * beta * summed(sums3, 2)
        + beta * beta * summed(sums3, 3)
    )
    factor = math.sqrt(secs * width * width) / jnp.sqrt(jnp.maximum(united_sq, 0.0) + eps)

    def finish(i, _):
        united = first * vec[chunk(i)].astype(jnp.float32) - beta * start[chunk(i)].astype(jnp.float32)
        ground_ref[chunk(i)] = (united * factor).astype(jnp.bfloat16)
        return 0

    lax.fori_loop(0, CHUNKS, finish, 0)

    for i in range(CHUNKS):
        x_copy(0, i, start_z, start_x).wait_send()
        x_copy(1, i, resid_z, resid_x).wait_send()
        z_copy(1, i, resid, resid_z).wait_send()
    for k in range(3):
        env_copy(k).wait_send()


def lanczos(table, psi, site, terms, right, secs):
    width = psi.shape[0]
    square = (width, width)
    bf = functools.partial(pltpu.VMEM, dtype=jnp.bfloat16)
    blocks = lambda *lead: pltpu.VMEM((*lead, *square), jnp.bfloat16)
    wide = pltpu.VMEM(square, jnp.float32)
    sums = pltpu.VMEM((secs, 8, 128), jnp.float32)
    dma = pltpu.SemaphoreType.DMA
    vmem = pl.BlockSpec(memory_space=pltpu.VMEM)
    return pl.pallas_call(
        lanczos_kernel,
        out_shape=jax.ShapeDtypeStruct(square, jnp.bfloat16),
        in_specs=[pl.BlockSpec(memory_space=pltpu.SMEM)] + [vmem] * 4,
        out_specs=vmem,
        scratch_shapes=[
            blocks(), blocks(), blocks(), blocks(), blocks(), blocks(3), blocks(3),
            blocks(), blocks(), blocks(), blocks(), blocks(), wide,
            blocks(), blocks(), blocks(), wide, wide,
            sums, sums, sums,
            dma((2, CHUNKS)), dma((2, CHUNKS)), dma((2, CHUNKS)), dma((2, CHUNKS)),
            dma((3,)), dma((3,)), dma((3, secs)), dma((3, secs)),
        ],
        compiler_params=pltpu.CompilerParams(
            collective_id=1, has_side_effects=True, vmem_limit_bytes=40 * 2**20
        ),
        cost_estimate=pl.CostEstimate(flops=16 * 2 * width**3, bytes_accessed=8 * width**2, transcendentals=0),
    )(table, psi, site, terms, right)


def fdot(left, right):
    return jnp.dot(left, right, precision=lax.Precision.HIGHEST, preferred_element_type=jnp.float32)


def spread_lane(tile, lane):
    return jnp.broadcast_to(tile[:, lane : lane + 1], tile.shape)


def spread_row(tile, row):
    return jnp.broadcast_to(tile[row : row + 1, :], tile.shape)


def invert_factor(block, panel):
    size = block.shape[0]
    count = size // 8
    tiles = [block[8 * t : 8 * t + 8] for t in range(count)]
    lane = lax.broadcasted_iota(jnp.int32, (8, size), 1)
    sub = lax.broadcasted_iota(jnp.int32, (8, size), 0)
    scales = [None] * count
    for j in range(0, size, panel):
        top, base = j // 8, j % 8
        cols = [
            {t: spread_lane(tiles[t], j + c) for t in range(top, count)} for c in range(panel)
        ]
        inside = (lane >= j) & (lane < j + panel)
        for t in range(top, count):
            tiles[t] = jnp.where(inside, jnp.where((lane - j == sub + 8 * t - j) , 1.0, 0.0) if t == top else 0.0, tiles[t])
        for c in range(panel):
            row = base + c
            pivot = spread_row(cols[c][top], row)
            inverse = 1.0 / pivot
            scale = lax.rsqrt(pivot)
            scales[top] = scale if scales[top] is None else jnp.where(sub >= row, scale, scales[top])
            below = sub > row
            factor = {}
            for t in range(top, count):
                f = cols[c][t] * inverse
                factor[t] = jnp.where(below, f, 0.0) if t == top else f
            for d in range(c + 1, panel):
                head = spread_row(cols[d][top], row)
                for t in range(top, count):
                    cols[d][t] = cols[d][t] - factor[t] * head
            line = spread_row(tiles[top], row)
            for t in range(top, count):
                tiles[t] = tiles[t] - factor[t] * line
    out = [tiles[t] * scales[t] for t in range(count)]
    full = jnp.concatenate(out, axis=0)
    r = lax.broadcasted_iota(jnp.int32, (size, size), 0)
    q = lax.broadcasted_iota(jnp.int32, (size, size), 1)
    return jnp.where(r >= q, full, 0.0)


def split_dot(left, right):
    result = None
    rest = left
    for _ in range(3):
        part = rest.astype(jnp.bfloat16)
        rest = rest - part.astype(jnp.float32)
        term = dot(part, right)
        result = term if result is None else result + term
    return result


def truncate_kernel(table_ref, ground_ref, cols_ref, kept_ref, dens_ref, basis, basis_t, range_t, gram, inv):
    width, rank = cols_ref.shape
    half = rank // 2
    lane = lax.broadcasted_iota(jnp.int32, (1, rank), 1)
    keep = jnp.where(lane < table_ref[0, 2], 1.0, 0.0)
    for b in range(2):
        block = pl.ds(b * 256, 256)
        rng = (dot(ground_ref[block], cols_ref[...]) * keep).astype(jnp.bfloat16)
        basis[block] = rng
        range_t[:, block] = rng.T
    row = lax.broadcasted_iota(jnp.int32, (rank, rank), 0)
    col = lax.broadcasted_iota(jnp.int32, (rank, rank), 1)
    gram[...] = dot(range_t[...], basis[...]) + jnp.where((row == col) & (col >= table_ref[0, 2]), 1.0, 0.0)
    first = invert_factor(gram[:half, :half], 8)
    upper = fdot(first, gram[:half, half:])
    upper_t = upper.T
    second = invert_factor(gram[half:, half:] - fdot(upper_t, upper), 8)
    inv[:half, :half] = first
    inv[:half, half:] = jnp.zeros((half, half), jnp.float32)
    inv[half:, :half] = -fdot(second, fdot(upper_t, first))
    inv[half:, half:] = second
    basis_t[...] = split_dot(inv[...], range_t[...]).astype(jnp.bfloat16)
    basis[...] = basis_t[...].T
    coeff = dot(basis_t[...], ground_ref[...]).astype(jnp.bfloat16)
    for b in range(2):
        block = pl.ds(b * 256, 256)
        kept_ref[block] = dot(basis[block], coeff).astype(jnp.bfloat16)
    kept_t = kept_ref[...].T
    for b in range(2):
        block = pl.ds(b * 256, 256)
        dens_ref[block] = (dot(kept_ref[block], kept_t) * (1.0 / width)).astype(jnp.bfloat16)


def truncate(table, ground, cols):
    width, rank = cols.shape
    square = jax.ShapeDtypeStruct((width, width), jnp.bfloat16)
    vmem = pl.BlockSpec(memory_space=pltpu.VMEM)
    return pl.pallas_call(
        truncate_kernel,
        out_shape=(square, square),
        in_specs=[pl.BlockSpec(memory_space=pltpu.SMEM), vmem, vmem],
        out_specs=(vmem, vmem),
        scratch_shapes=[
            pltpu.VMEM((width, rank), jnp.bfloat16),
            pltpu.VMEM((rank, width), jnp.bfloat16),
            pltpu.VMEM((rank, width), jnp.bfloat16),
            pltpu.VMEM((rank, rank), jnp.float32),
            pltpu.VMEM((rank, rank), jnp.float32),
        ],
        compiler_params=pltpu.CompilerParams(vmem_limit_bytes=24 * 2**20),
        cost_estimate=pl.CostEstimate(flops=2 * width**3 * 3, bytes_accessed=3 * width**2, transcendentals=0),
    )(table, ground, cols)


def per_device(psi_start, left_site, left_terms, right_terms, start_cols, sector_table):
    ground = lanczos(
        sector_table, psi_start[0, 0], left_site[0, 0], left_terms[0, 0], right_terms[0, 0],
        lax.axis_size("sec"),
    )
    kept, dens = truncate(sector_table, ground, start_cols[0])
    segs = lax.axis_size("seg")
    back = lax.ppermute(dens, "seg", [(i + 1, i) for i in range(segs - 1)])
    return (kept[None, None], back[None, None])


def solution(mesh):
    placed = (
        P("seg", "sec", None, None),
        P("seg", "sec", None, None),
        P("seg", "sec", None, None, None),
        P("seg", "sec", None, None, None),
        P("sec", None, None),
        P("sec", None),
    )
    return jax.shard_map(
        per_device,
        mesh=mesh,
        in_specs=placed,
        out_specs=(P("seg", "sec", None, None), P("seg", "sec", None, None)),
        check_vma=False,
    )
```

```python
import math

import jax
import jax.numpy as jnp
from jax import lax
from jax.experimental import pallas as pl
from jax.experimental.pallas import tpu as pltpu
from jax.sharding import PartitionSpec as P

eps = 1e-06
MESH = pl.DeviceIdType.MESH
CHUNKS = 8
ENV_AT = 4
AHEAD = 1


def dot(left, right):
    return jnp.dot(left, right, preferred_element_type=jnp.float32)


def dot_left_t(left, right):
    return lax.dot_general(
        left, right, (((0,), (0,)), ((), ())), preferred_element_type=jnp.float32
    )


def dot_right_t(left, right):
    return lax.dot_general(
        left, right, (((1,), (1,)), ((), ())), preferred_element_type=jnp.float32
    )


def total(block):
    return jnp.sum(jnp.sum(block, axis=0, keepdims=True), axis=1, keepdims=True)


def pack(values):
    lane = lax.broadcasted_iota(jnp.int32, (1, 128), 1)
    row = jnp.zeros((1, 128), jnp.float32)
    for k, value in enumerate(values):
        row = jnp.where(lane == k, value, row)
    return row


def lanczos_kernel(
    table_ref, psi_hbm, site_hbm, terms_hbm, right_hbm, ground_ref,
    psi, site, terms, right,
    start, start_z, start_x, site_t, part, built, env, vec, vec_z,
    low_z, low_x, image, resid, resid_z, ritz, adj, pull, pull_out, pull_in,
    sums1, sums2, sums3,
    load, z_send, z_recv, x_send, x_recv, env_send, env_recv, pull_send, pull_recv, sum_send, sum_recv,
):
    seg, sec = lax.axis_index("seg"), lax.axis_index("sec")
    segs, secs = lax.axis_size("seg"), lax.axis_size("sec")
    width = psi.shape[0]
    rows = width // CHUNKS
    half = width // 2
    parity = lax.rem(sec, 2)
    partner = sec + 1 - 2 * parity
    relay = lax.rem(sec + 2 - 4 * parity + secs, secs)
    source = lax.rem(sec - 2 + 4 * parity + secs, secs)
    nxt, prv = lax.rem(seg + 1, segs), lax.rem(seg + segs - 1, segs)
    peers = [(seg, lax.rem(sec + d, secs)) for d in range(1, secs)]

    barrier = pltpu.get_barrier_semaphore()
    neighbours = peers + [(nxt, sec), (prv, sec)]
    for device in neighbours:
        pl.semaphore_signal(barrier, inc=1, device_id=device, device_id_type=MESH)

    loads = [
        pltpu.make_async_copy(psi_hbm, psi, load.at[0]),
        pltpu.make_async_copy(site_hbm, site, load.at[1]),
        pltpu.make_async_copy(terms_hbm, terms, load.at[2]),
        pltpu.make_async_copy(right_hbm, right, load.at[3]),
    ]
    for copy in loads:
        copy.start()

    def chunk(i):
        return pl.ds(pl.multiple_of(i * rows, rows), rows)

    def halves(b):
        return pl.ds(pl.multiple_of(b * half, half), half)

    def z_copy(phase, i, held, target):
        return pltpu.make_async_remote_copy(
            held.at[chunk(i)], target.at[chunk(i)],
            z_send.at[phase, i], z_recv.at[phase, i],
            device_id=(seg, partner), device_id_type=MESH,
        )

    def x_copy(i):
        return pltpu.make_async_remote_copy(
            start_z.at[chunk(i)], start_x.at[chunk(i)],
            x_send.at[i], x_recv.at[i],
            device_id=(seg, relay), device_id_type=MESH,
        )

    def env_copy(i):
        return pltpu.make_async_remote_copy(
            built.at[:, chunk(i)], env.at[:, chunk(i)], env_send.at[i], env_recv.at[i],
            device_id=(nxt, sec), device_id_type=MESH,
        )

    def pull_copy():
        return pltpu.make_async_remote_copy(
            pull_out, pull_in, pull_send.at[0], pull_recv.at[0],
            device_id=(seg, source), device_id_type=MESH,
        )

    def sum_copies(phase, buffer):
        return [
            pltpu.make_async_remote_copy(
                buffer.at[sec], buffer.at[sec],
                sum_send.at[phase, d], sum_recv.at[phase, d],
                device_id=peers[d], device_id_type=MESH,
            )
            for d in range(secs - 1)
        ]

    def share(phase, buffer):
        for copy in sum_copies(phase, buffer):
            copy.start()

    def collect(phase, buffer):
        for copy in sum_copies(phase, buffer):
            copy.wait()

    def summed(buffer):
        return jnp.sum(jnp.sum(buffer[...], axis=0), axis=0, keepdims=True)

    live_rows, live_cols = table_ref[0, 0], table_ref[0, 1]

    def mask(first, count):
        i = lax.broadcasted_iota(jnp.int32, (count, width), 0) + first
        j = lax.broadcasted_iota(jnp.int32, (count, width), 1)
        return (i < live_rows) & (j < live_cols)

    zero = jnp.zeros((1, 1), jnp.float32)
    blank = jnp.zeros((8, 128), jnp.float32)
    sums1[sec] = blank
    sums3[sec] = blank
    loads[0].wait()

    def begin(i, norm):
        piece = jnp.where(mask(i * rows, rows), psi[chunk(i)].astype(jnp.float32), 0.0)
        start[chunk(i)] = piece.astype(jnp.bfloat16)
        return norm + total(piece * piece)

    norm = lax.fori_loop(0, CHUNKS, begin, zero)
    sums1[sec, pl.ds(0, 1)] = pack([norm])

    pl.semaphore_wait(barrier, len(neighbours))

    share(0, sums1)

    def send_start(i, _):
        z_copy(0, i, start, start_z).start()
        return 0

    lax.fori_loop(0, CHUNKS, send_start, 0)

    loads[1].wait()
    site_t[...] = site[...].T
    loads[2].wait()

    def build(k, _):
        def left(b, _):
            part[halves(b)] = dot(terms[k, halves(b)], site[...]).astype(jnp.bfloat16)
            return 0

        lax.fori_loop(0, 2, left, 0)

        def outer(b, _):
            built[k, halves(b)] = dot(site_t[halves(b)], part[...]).astype(jnp.bfloat16)
            return 0

        lax.fori_loop(0, 2, outer, 0)
        return 0

    lax.fori_loop(0, 3, build, 0)

    loads[3].wait()
    collect(0, sums1)
    scale = 1.0 / jnp.sqrt(summed(sums1)[:, 0:1] + eps)
    has_env = jnp.where(seg > 0, 1.0, 0.0).astype(jnp.float32)
    has_x = jnp.where((sec > 0) & (sec < secs - 1), 1.0, 0.0).astype(jnp.float32)

    def scaled(i, held):
        return (held[chunk(i)].astype(jnp.float32) * scale).astype(jnp.bfloat16)

    def own(i, _):
        vec[chunk(i)] = scaled(i, start)
        return 0

    lax.fori_loop(0, CHUNKS, own, 0)

    right_z, right_x = right.at[1 - parity], right.at[parity]
    env_z, env_x = env.at[2 - parity], env.at[1 + parity]

    def first_z(i):
        z_copy(0, i, start, start_z).wait_recv()
        x_copy(i).start()
        piece = scaled(i, start_z)
        vec_z[chunk(i)] = piece
        low_z[chunk(i)] = dot(piece, right_z[...]).astype(jnp.bfloat16)

    def first_x(i):
        x_copy(i).wait_recv()
        low_x[chunk(i)] = (dot(scaled(i, start_x), right_x[...]) * has_x).astype(jnp.bfloat16)

    def arrive(i, _):
        first_z(i)
        first_x(i - 1)
        return 0

    def arrive_send(i, _):
        env_copy(i - ENV_AT).start()
        return arrive(i, 0)

    first_z(0)
    lax.fori_loop(1, ENV_AT, arrive, 0)
    lax.fori_loop(ENV_AT, CHUNKS, arrive_send, 0)

    def send_env(i, _):
        env_copy(i).start()
        return 0

    lax.fori_loop(CHUNKS - ENV_AT, CHUNKS, send_env, 0)
    first_x(CHUNKS - 1)

    def apply(i, _):
        env_copy(i).wait_recv()
        value = dot(env[0, chunk(i)], vec[...])
        value += dot(env_z[chunk(i)], low_z[...])
        value += dot(env_x[chunk(i)], low_x[...])
        value = jnp.where(mask(i * rows, rows), value * has_env, 0.0)
        mine = vec[chunk(i)].astype(jnp.float32)
        along, size = total(mine * value), total(mine * mine)
        ratio = jnp.where(size > 0.0, along / jnp.where(size > 0.0, size, 1.0), 0.0)
        piece = value - ratio * mine
        image[chunk(i)] = piece
        resid[chunk(i)] = piece.astype(jnp.bfloat16)
        sums2[sec, pl.ds(i, 1)] = pack([along, size, total(piece * piece), total(mine * piece), ratio])
        return 0

    def send_resid(i, _):
        z_copy(1, i, resid, resid_z).start()
        return 0

    def apply_send(i, _):
        apply(i, 0)
        return send_resid(i, 0)

    lax.fori_loop(0, AHEAD, apply_send, 0)
    lax.fori_loop(AHEAD, CHUNKS, apply, 0)
    share(1, sums2)
    lax.fori_loop(AHEAD, CHUNKS, send_resid, 0)
    collect(1, sums2)

    totals = summed(sums2)
    alpha, size = totals[:, 0:1], totals[:, 1:2]
    beta_sq = zero
    for s in range(secs):
        tile = sums2[s]
        delta = tile[:, 4:5] - alpha
        beta_sq = beta_sq + total(tile[:, 2:3] + 2.0 * delta * tile[:, 3:4] + delta * delta * tile[:, 1:2])
    beta = jnp.sqrt(jnp.maximum(beta_sq, 0.0) + eps)
    inverse = 1.0 / beta

    def shift(s, i):
        return sums2[s, pl.ds(i, 1)][:, 4:5] - alpha

    def second(i, sums):
        mine = vec[chunk(i)].astype(jnp.float32)
        piece = ((image[chunk(i)] + shift(sec, i) * mine) * inverse).astype(jnp.bfloat16)
        ritz[chunk(i)] = piece
        wide = piece.astype(jnp.float32)
        return sums[0] + total(mine * wide), sums[1] + total(wide * wide)

    overlap, size2 = lax.fori_loop(0, CHUNKS, second, (zero, zero))

    for b in range(2):
        adj[b * half : (b + 1) * half] = dot_left_t(env_x[:, b * half : (b + 1) * half], ritz[...]).astype(jnp.bfloat16)

    def pull_x(b, _):
        pull_out[halves(b)] = (dot_right_t(adj[halves(b)], right_x[...]) * has_x).astype(jnp.bfloat16)
        return 0

    lax.fori_loop(0, 2, pull_x, 0)
    pull_copy().start()
    for b in range(2):
        adj[b * half : (b + 1) * half] = dot_left_t(env_z[:, b * half : (b + 1) * half], ritz[...]).astype(jnp.bfloat16)

    def pull_z(b, gamma):
        pull[halves(b)] = dot_right_t(adj[halves(b)], right_z[...])
        return gamma + total(ritz[halves(b)].astype(jnp.float32) * dot(env[0, halves(b)], ritz[...]))

    gamma = lax.fori_loop(0, 2, pull_z, zero)
    pull_copy().wait_recv()

    def join(i, partial):
        both = pull[chunk(i)] + pull_in[chunk(i)].astype(jnp.float32)
        pull[chunk(i)] = both
        return partial + shift(partner, i) * total(both * vec_z[chunk(i)].astype(jnp.float32))

    cross = lax.fori_loop(0, CHUNKS, join, zero)

    def meet(i, partial):
        z_copy(1, i, resid, resid_z).wait_recv()
        return partial + total(pull[chunk(i)] * resid_z[chunk(i)].astype(jnp.float32))

    cross = lax.fori_loop(0, CHUNKS, meet, cross)
    gamma = (gamma + cross * inverse) * has_env
    sums3[sec, pl.ds(0, 1)] = pack([gamma, overlap, size2])
    share(2, sums3)
    collect(2, sums3)
    totals = summed(sums3)
    gamma = totals[:, 0:1]
    lowest = 0.5 * (alpha + gamma) - jnp.sqrt(0.25 * (alpha - gamma) ** 2 + beta * beta)
    first = gamma - lowest
    united_sq = (
        first * first * size - 2.0 * first * beta * totals[:, 1:2] + beta * beta * totals[:, 2:3]
    )
    factor = math.sqrt(secs * width * width) / jnp.sqrt(jnp.maximum(united_sq, 0.0) + eps)

    def finish(i, _):
        united = first * vec[chunk(i)].astype(jnp.float32) - beta * ritz[chunk(i)].astype(jnp.float32)
        ground_ref[chunk(i)] = (united * factor).astype(jnp.bfloat16)
        return 0

    lax.fori_loop(0, CHUNKS, finish, 0)

    def drain(i, _):
        z_copy(0, i, start, start_z).wait_send()
        z_copy(1, i, resid, resid_z).wait_send()
        x_copy(i).wait_send()
        env_copy(i).wait_send()
        return 0

    lax.fori_loop(0, CHUNKS, drain, 0)
    pull_copy().wait_send()


def lanczos(table, psi, site, terms, right, secs):
    width = psi.shape[0]
    square = (width, width)
    blocks = lambda *lead: pltpu.VMEM((*lead, *square), jnp.bfloat16)
    wide = pltpu.VMEM(square, jnp.float32)
    sums = pltpu.VMEM((secs, 8, 128), jnp.float32)
    dma = pltpu.SemaphoreType.DMA
    return pl.pallas_call(
        lanczos_kernel,
        out_shape=jax.ShapeDtypeStruct(square, jnp.bfloat16),
        in_specs=[pl.BlockSpec(memory_space=pltpu.SMEM)] + [pl.BlockSpec(memory_space=pl.ANY)] * 4,
        out_specs=pl.BlockSpec(memory_space=pltpu.VMEM),
        scratch_shapes=[
            blocks(), blocks(), blocks(3), blocks(2),
            blocks(), blocks(), blocks(), blocks(), blocks(), blocks(3), blocks(3), blocks(), blocks(),
            blocks(), blocks(), wide, blocks(), blocks(), blocks(), blocks(), wide, blocks(), blocks(),
            sums, sums, sums,
            dma((4,)), dma((2, CHUNKS)), dma((2, CHUNKS)), dma((CHUNKS,)), dma((CHUNKS,)),
            dma((CHUNKS,)), dma((CHUNKS,)), dma((1,)), dma((1,)), dma((3, secs)), dma((3, secs)),
        ],
        compiler_params=pltpu.CompilerParams(
            collective_id=1, has_side_effects=True, vmem_limit_bytes=62 * 2**20
        ),
        cost_estimate=pl.CostEstimate(flops=16 * 2 * width**3, bytes_accessed=8 * width**2, transcendentals=0),
    )(table, psi, site, terms, right)


def fdot(left, right):
    return jnp.dot(left, right, precision=lax.Precision.HIGHEST, preferred_element_type=jnp.float32)


def spread_lane(tile, lane):
    return jnp.broadcast_to(tile[:, lane : lane + 1], tile.shape)


def spread_row(tile, row):
    return jnp.broadcast_to(tile[row : row + 1, :], tile.shape)


def invert_factor(block, panel):
    size = block.shape[0]
    count = size // 8
    tiles = [block[8 * t : 8 * t + 8] for t in range(count)]
    lane = lax.broadcasted_iota(jnp.int32, (8, size), 1)
    sub = lax.broadcasted_iota(jnp.int32, (8, size), 0)
    scales = [None] * count
    for j in range(0, size, panel):
        top, base = j // 8, j % 8
        cols = [
            {t: spread_lane(tiles[t], j + c) for t in range(top, count)} for c in range(panel)
        ]
        inside = (lane >= j) & (lane < j + panel)
        for t in range(top, count):
            tiles[t] = jnp.where(inside, jnp.where((lane - j == sub + 8 * t - j) , 1.0, 0.0) if t == top else 0.0, tiles[t])
        for c in range(panel):
            row = base + c
            pivot = spread_row(cols[c][top], row)
            inverse = 1.0 / pivot
            scale = lax.rsqrt(pivot)
            scales[top] = scale if scales[top] is None else jnp.where(sub >= row, scale, scales[top])
            below = sub > row
            factor = {}
            for t in range(top, count):
                f = cols[c][t] * inverse
                factor[t] = jnp.where(below, f, 0.0) if t == top else f
            for d in range(c + 1, panel):
                head = spread_row(cols[d][top], row)
                for t in range(top, count):
                    cols[d][t] = cols[d][t] - factor[t] * head
            line = spread_row(tiles[top], row)
            for t in range(top, count):
                tiles[t] = tiles[t] - factor[t] * line
    out = [tiles[t] * scales[t] for t in range(count)]
    full = jnp.concatenate(out, axis=0)
    r = lax.broadcasted_iota(jnp.int32, (size, size), 0)
    q = lax.broadcasted_iota(jnp.int32, (size, size), 1)
    return jnp.where(r >= q, full, 0.0)


def split_dot(left, right):
    result = None
    rest = left
    for _ in range(3):
        part = rest.astype(jnp.bfloat16)
        rest = rest - part.astype(jnp.float32)
        term = dot(part, right)
        result = term if result is None else result + term
    return result


def truncate_kernel(table_ref, ground_ref, cols_ref, kept_ref, dens_ref, basis, basis_t, range_t, gram, inv):
    width, rank = cols_ref.shape
    half = rank // 2
    lane = lax.broadcasted_iota(jnp.int32, (1, rank), 1)
    keep = jnp.where(lane < table_ref[0, 2], 1.0, 0.0)
    for b in range(2):
        block = pl.ds(b * 256, 256)
        rng = (dot(ground_ref[block], cols_ref[...]) * keep).astype(jnp.bfloat16)
        basis[block] = rng
        range_t[:, block] = rng.T
    row = lax.broadcasted_iota(jnp.int32, (rank, rank), 0)
    col = lax.broadcasted_iota(jnp.int32, (rank, rank), 1)
    gram[...] = dot(range_t[...], basis[...]) + jnp.where((row == col) & (col >= table_ref[0, 2]), 1.0, 0.0)
    first = invert_factor(gram[:half, :half], 8)
    upper = fdot(first, gram[:half, half:])
    upper_t = upper.T
    second = invert_factor(gram[half:, half:] - fdot(upper_t, upper), 8)
    inv[:half, :half] = first
    inv[:half, half:] = jnp.zeros((half, half), jnp.float32)
    inv[half:, :half] = -fdot(second, fdot(upper_t, first))
    inv[half:, half:] = second
    basis_t[...] = split_dot(inv[...], range_t[...]).astype(jnp.bfloat16)
    basis[...] = basis_t[...].T
    coeff = dot(basis_t[...], ground_ref[...]).astype(jnp.bfloat16)
    for b in range(2):
        block = pl.ds(b * 256, 256)
        kept_ref[block] = dot(basis[block], coeff).astype(jnp.bfloat16)
    kept_t = kept_ref[...].T
    for b in range(2):
        block = pl.ds(b * 256, 256)
        dens_ref[block] = (dot(kept_ref[block], kept_t) * (1.0 / width)).astype(jnp.bfloat16)


def truncate(table, ground, cols):
    width, rank = cols.shape
    square = jax.ShapeDtypeStruct((width, width), jnp.bfloat16)
    vmem = pl.BlockSpec(memory_space=pltpu.VMEM)
    return pl.pallas_call(
        truncate_kernel,
        out_shape=(square, square),
        in_specs=[pl.BlockSpec(memory_space=pltpu.SMEM), vmem, vmem],
        out_specs=(vmem, vmem),
        scratch_shapes=[
            pltpu.VMEM((width, rank), jnp.bfloat16),
            pltpu.VMEM((rank, width), jnp.bfloat16),
            pltpu.VMEM((rank, width), jnp.bfloat16),
            pltpu.VMEM((rank, rank), jnp.float32),
            pltpu.VMEM((rank, rank), jnp.float32),
        ],
        compiler_params=pltpu.CompilerParams(vmem_limit_bytes=24 * 2**20),
        cost_estimate=pl.CostEstimate(flops=2 * width**3 * 3, bytes_accessed=3 * width**2, transcendentals=0),
    )(table, ground, cols)


def per_device(psi_start, left_site, left_terms, right_terms, start_cols, sector_table):
    ground = lanczos(
        sector_table, psi_start[0, 0], left_site[0, 0], left_terms[0, 0], right_terms[0, 0],
        lax.axis_size("sec"),
    )
    kept, dens = truncate(sector_table, ground, start_cols[0])
    segs = lax.axis_size("seg")
    back = lax.ppermute(dens, "seg", [(i + 1, i) for i in range(segs - 1)])
    return (kept[None, None], back[None, None])


def solution(mesh):
    placed = (
        P("seg", "sec", None, None),
        P("seg", "sec", None, None),
        P("seg", "sec", None, None, None),
        P("seg", "sec", None, None, None),
        P("sec", None, None),
        P("sec", None),
    )
    return jax.shard_map(
        per_device,
        mesh=mesh,
        in_specs=placed,
        out_specs=(P("seg", "sec", None, None), P("seg", "sec", None, None)),
        check_vma=False,
    )
```

```python
import math

import jax
import jax.numpy as jnp
from jax import lax
from jax.experimental import pallas as pl
from jax.experimental.pallas import tpu as pltpu
from jax.sharding import PartitionSpec as P

eps = 1e-06
MESH = pl.DeviceIdType.MESH
CHUNKS = 8
ENV_AT = 1
LEG = 4


def dot(left, right):
    return jnp.dot(left, right, preferred_element_type=jnp.float32)


def dot_left_t(left, right):
    return lax.dot_general(
        left, right, (((0,), (0,)), ((), ())), preferred_element_type=jnp.float32
    )


def dot_right_t(left, right):
    return lax.dot_general(
        left, right, (((1,), (1,)), ((), ())), preferred_element_type=jnp.float32
    )


def total(block):
    return jnp.sum(jnp.sum(block, axis=0, keepdims=True), axis=1, keepdims=True)


def pack(values):
    lane = lax.broadcasted_iota(jnp.int32, (1, 128), 1)
    row = jnp.zeros((1, 128), jnp.float32)
    for k, value in enumerate(values):
        row = jnp.where(lane == k, value, row)
    return row


def lanczos_kernel(
    table_ref, psi_hbm, site_hbm, terms_hbm, right_hbm, ground_ref,
    psi, site, terms, right,
    start, start_z, start_x, site_t, part, built, env, vec, vec_z,
    held, low_z, low_x, image, resid, resid_z, adj, pull, pull_out, pull_in,
    sums1, sums2, deltas,
    load, a_send, a_recv, z_send, z_recv, x_send, x_recv, env_send, env_recv, pull_send, pull_recv, sum_send, sum_recv,
):
    seg, sec = lax.axis_index("seg"), lax.axis_index("sec")
    segs, secs = lax.axis_size("seg"), lax.axis_size("sec")
    width = psi.shape[0]
    rows = width // CHUNKS
    half = width // 2
    parity = lax.rem(sec, 2)
    partner = sec + 1 - 2 * parity
    relay = lax.rem(sec + 2 - 4 * parity + secs, secs)
    source = lax.rem(sec - 2 + 4 * parity + secs, secs)
    nxt, prv = lax.rem(seg + 1, segs), lax.rem(seg + segs - 1, segs)
    core, z_lo, line = lax.rem(seg, 2), lax.rem(lax.div(seg, 2), 8), lax.div(seg, 16)

    def along_z(distance):
        place = lax.rem(parity * 8 + z_lo + distance, 16)
        return ((line * 8 + lax.rem(place, 8)) * 2 + core, sec - parity + lax.div(place, 8))

    peers = [(seg, lax.rem(sec + d, secs)) for d in range(1, secs)]

    barrier = pltpu.get_barrier_semaphore()
    neighbours = peers + [(nxt, sec), (prv, sec), along_z(LEG), along_z(16 - LEG)]
    for device in neighbours:
        pl.semaphore_signal(barrier, inc=1, device_id=device, device_id_type=MESH)

    loads = [
        pltpu.make_async_copy(psi_hbm, psi, load.at[0]),
        pltpu.make_async_copy(site_hbm, site, load.at[1]),
        pltpu.make_async_copy(terms_hbm, terms, load.at[2]),
        pltpu.make_async_copy(right_hbm, right, load.at[3]),
    ]
    for copy in loads:
        copy.start()

    def chunk(i):
        return pl.ds(pl.multiple_of(i * rows, rows), rows)

    def halves(b):
        return pl.ds(pl.multiple_of(b * half, half), half)

    def leg(i):
        return along_z(LEG + lax.rem(i, 2) * (16 - 2 * LEG))

    def a_copy(phase, i, block):
        return pltpu.make_async_remote_copy(
            block.at[chunk(i)], (start_z, resid_z)[phase].at[chunk(i)],
            a_send.at[phase, i], a_recv.at[phase, i],
            device_id=(seg, partner), device_id_type=MESH,
        )

    def z_copy(phase, i, target):
        return a_copy(phase, i, (start, resid)[phase])

    def forward(phase, i, block, target):
        return

    def forward_two(phase, j, block, target):
        forward(phase, 2 * j, block, target)
        forward(phase, 2 * j + 1, block, target)

    def x_copy(i):
        return pltpu.make_async_remote_copy(
            start_z.at[chunk(i)], start_x.at[chunk(i)],
            x_send.at[i], x_recv.at[i],
            device_id=(seg, relay), device_id_type=MESH,
        )

    def env_copy(i):
        return pltpu.make_async_remote_copy(
            built.at[:, chunk(i)], env.at[:, chunk(i)], env_send.at[i], env_recv.at[i],
            device_id=(nxt, sec), device_id_type=MESH,
        )

    def pull_copy(k):
        return pltpu.make_async_remote_copy(
            pull_out.at[k], pull_in.at[k], pull_send.at[k], pull_recv.at[k],
            device_id=(seg, source), device_id_type=MESH,
        )

    def sum_copies(phase, buffer):
        return [
            pltpu.make_async_remote_copy(
                buffer.at[sec], buffer.at[sec],
                sum_send.at[phase, d], sum_recv.at[phase, d],
                device_id=peers[d], device_id_type=MESH,
            )
            for d in range(secs - 1)
        ]

    def share(phase, buffer):
        for copy in sum_copies(phase, buffer):
            copy.start()

    def collect(phase, buffer):
        for copy in sum_copies(phase, buffer):
            copy.wait()

    def summed(buffer):
        return jnp.sum(jnp.sum(buffer[...], axis=0), axis=0, keepdims=True)

    live_rows, live_cols = table_ref[0, 0], table_ref[0, 1]

    def mask(first, count):
        i = lax.broadcasted_iota(jnp.int32, (count, width), 0) + first
        j = lax.broadcasted_iota(jnp.int32, (count, width), 1)
        return (i < live_rows) & (j < live_cols)

    zero = jnp.zeros((1, 1), jnp.float32)
    blank = jnp.zeros((8, 128), jnp.float32)
    sums1[sec] = blank
    sums2[sec] = blank
    loads[0].wait()

    def begin(i, norm):
        piece = jnp.where(mask(i * rows, rows), psi[chunk(i)].astype(jnp.float32), 0.0)
        start[chunk(i)] = piece.astype(jnp.bfloat16)
        return norm + total(piece * piece)

    norm = lax.fori_loop(0, CHUNKS, begin, zero)
    sums1[sec, pl.ds(0, 1)] = pack([norm])

    pl.semaphore_wait(barrier, len(neighbours))

    share(0, sums1)

    def send_start(i, _):
        a_copy(0, i, start).start()
        return 0

    lax.fori_loop(0, CHUNKS, send_start, 0)

    loads[1].wait()
    site_t[...] = site[...].T
    loads[2].wait()

    def build(k, _):
        def left(b, _):
            part[halves(b)] = dot(terms[k, halves(b)], site[...]).astype(jnp.bfloat16)
            return 0

        lax.fori_loop(0, 2, left, 0)

        def outer(b, _):
            built[k, halves(b)] = dot(site_t[halves(b)], part[...]).astype(jnp.bfloat16)
            return 0

        lax.fori_loop(0, 2, outer, 0)
        return 0

    lax.fori_loop(0, 3, build, 0)

    loads[3].wait()
    forward_two(0, 0, start, start_z)
    collect(0, sums1)
    scale = 1.0 / jnp.sqrt(summed(sums1)[:, 0:1] + eps)
    has_env = jnp.where(seg > 0, 1.0, 0.0).astype(jnp.float32)
    has_x = jnp.where((sec > 0) & (sec < secs - 1), 1.0, 0.0).astype(jnp.float32)

    def scaled(i, held):
        return (held[chunk(i)].astype(jnp.float32) * scale).astype(jnp.bfloat16)

    def own(i, _):
        vec[chunk(i)] = scaled(i, start)
        return 0

    lax.fori_loop(0, CHUNKS, own, 0)

    right_z, right_x = right.at[1 - parity], right.at[parity]
    env_z, env_x = env.at[2 - parity], env.at[1 + parity]

    def first_z(i):
        z_copy(0, i, start_z).wait_recv()
        x_copy(i).start()
        piece = scaled(i, start_z)
        vec_z[chunk(i)] = piece
        low_z[chunk(i)] = dot(piece, right_z[...]).astype(jnp.bfloat16)

    def first_x(i):
        x_copy(i).wait_recv()
        low_x[chunk(i)] = (dot(scaled(i, start_x), right_x[...]) * has_x).astype(jnp.bfloat16)

    pairs = CHUNKS // 2

    def arrive(j, _):
        forward_two(0, j, start, start_z)
        first_z(2 * j - 2)
        first_z(2 * j - 1)

        @pl.when(j > 1)
        def _():
            first_x(2 * j - 4)
            first_x(2 * j - 3)

        return 0

    def send_env(i, _):
        env_copy(i).start()
        return 0

    def arrive_send(j, _):
        send_env(2 * (j - ENV_AT), 0)
        send_env(2 * (j - ENV_AT) + 1, 0)
        return arrive(j, 0)

    lax.fori_loop(1, ENV_AT, arrive, 0)
    lax.fori_loop(ENV_AT, pairs, arrive_send, 0)
    lax.fori_loop(2 * (pairs - ENV_AT), CHUNKS, send_env, 0)
    first_z(CHUNKS - 2)
    first_z(CHUNKS - 1)
    for i in range(CHUNKS - 4, CHUNKS):
        first_x(i)

    def image_of(i):
        env_copy(i).wait_recv()
        value = dot(env[0, chunk(i)], vec[...])
        value += dot(env_z[chunk(i)], low_z[...])
        value += dot(env_x[chunk(i)], low_x[...])
        return jnp.where(mask(i * rows, rows), value * has_env, 0.0)

    def emit(i, value, guess, sums):
        mine = vec[chunk(i)].astype(jnp.float32)
        piece = value - guess * mine
        image[chunk(i)] = piece
        resid[chunk(i)] = piece.astype(jnp.bfloat16)
        a_copy(1, i, resid).start()
        return sums[0] + total(mine * value), sums[1] + total(mine * mine)

    def quotient(along, size):
        return jnp.where(size > 0.0, along / jnp.where(size > 0.0, size, 1.0), 0.0)

    value = image_of(0)
    mine = vec[chunk(0)].astype(jnp.float32)
    guess = quotient(total(mine * value), total(mine * mine))
    sums = emit(0, value, guess, (zero, zero))

    def apply(i, sums):
        return emit(i, image_of(i), guess, sums)

    sums = lax.fori_loop(1, CHUNKS // 2, apply, sums)
    forward_two(1, 0, resid, resid_z)
    along, size = lax.fori_loop(CHUNKS // 2, CHUNKS, apply, sums)

    def turned(matrix, vector):
        for b in range(2):
            block = slice(b * half, (b + 1) * half)
            adj[block] = dot_left_t(matrix[:, block], vector[...]).astype(jnp.bfloat16)

    def pull_away(k, vector):
        turned(env_x, vector)

        def piece(b, _):
            pull_out[k, halves(b)] = (dot_right_t(adj[halves(b)], right_x[...]) * has_x).astype(jnp.bfloat16)
            return 0

        lax.fori_loop(0, 2, piece, 0)
        pull_copy(k).start()

    def pull_here(k, vector):
        turned(env_z, vector)

        def piece(b, _):
            pull[k, halves(b)] = dot_right_t(adj[halves(b)], right_z[...])
            return 0

        lax.fori_loop(0, 2, piece, 0)

    pull_away(0, resid)
    pull_away(1, vec)
    forward_two(1, 1, resid, resid_z)
    pull_here(0, resid)
    pull_here(1, vec)

    def diagonal(b, sums):
        image_r = dot(env[0, halves(b)], resid[...])
        image_v = dot(env[0, halves(b)], vec[...])
        mine_r, mine_v = resid[halves(b)].astype(jnp.float32), vec[halves(b)].astype(jnp.float32)
        return (
            sums[0] + total(mine_r * image_r),
            sums[1] + total(mine_r * image_v + mine_v * image_r),
            sums[2] + total(mine_v * image_v),
        )

    square_r, mixed, square_v = lax.fori_loop(0, 2, diagonal, (zero, zero, zero))
    ratio = quotient(along, size)

    def norms(i, sums):
        mine = vec[chunk(i)].astype(jnp.float32)
        piece = image[chunk(i)] + (guess - ratio) * mine
        return sums[0] + total(piece * piece), sums[1] + total(mine * piece)

    rho, cross = lax.fori_loop(0, CHUNKS, norms, (zero, zero))
    pull_copy(0).wait_recv()
    pull_copy(1).wait_recv()

    def join(i, sums):
        both = pull[0, chunk(i)] + pull_in[0, chunk(i)].astype(jnp.float32)
        pull[0, chunk(i)] = both
        base = vec_z[chunk(i)].astype(jnp.float32)
        return (
            sums[0] + total(both * base),
            sums[1] + total(pull[1, chunk(i)] * base),
            sums[2] + total(pull_in[1, chunk(i)].astype(jnp.float32) * base),
        )

    base_r, base_v, base_x = lax.fori_loop(0, CHUNKS, join, (zero, zero, zero))

    def meet(i, sums):
        z_copy(1, i, resid_z).wait_recv()
        other = resid_z[chunk(i)].astype(jnp.float32)
        terms = (pull[0, chunk(i)], pull[1, chunk(i)], pull_in[1, chunk(i)].astype(jnp.float32))
        return tuple(old + jnp.sum(term * other, axis=0, keepdims=True) for old, term in zip(sums, terms))

    def meet_two(j, sums):
        forward_two(1, j, resid, resid_z)
        return meet(2 * j - 3, meet(2 * j - 4, sums))

    line_sums = (jnp.zeros((1, width), jnp.float32),) * 3
    line_sums = lax.fori_loop(2, pairs, meet_two, line_sums)
    line_sums = lax.fori_loop(CHUNKS - 4, CHUNKS, meet, line_sums)
    met_r, met_v, met_x = [jnp.sum(line, axis=1, keepdims=True) for line in line_sums]
    sums2[sec, pl.ds(0, 1)] = pack(
        [along, size, rho, cross, ratio, guess]
        + [
            term * has_env
            for term in (square_r + met_r, mixed + met_v, square_v, met_x, base_r, base_v, base_x)
        ]
    )
    share(1, sums2)
    collect(1, sums2)

    gathered = jnp.sum(sums2[...], axis=1)
    column = lambda k: gathered[:, k : k + 1]
    over = lambda value: jnp.sum(value, axis=0, keepdims=True)
    alpha, size = over(column(0)), over(column(1))
    delta = column(4) - alpha
    resid_sq = jnp.maximum(over(column(2) + delta * (2.0 * column(3) + delta * column(1))), 0.0)
    overlap = over(column(3) + delta * column(1))
    beta_sq = resid_sq + eps
    beta = jnp.sqrt(beta_sq)
    inverse = 1.0 / beta
    own = column(5) - alpha
    deltas[...] = jnp.broadcast_to(own, deltas.shape)
    picked = lambda order: jnp.concatenate([deltas[s : s + 1] for s in order], axis=0)[:, 0:1]
    beside = picked([s + 1 - 2 * (s % 2) for s in range(secs)])
    across = picked([(s + 2 - 4 * (s % 2)) % secs for s in range(secs)])
    gamma = over(
        column(6) + own * (column(7) + own * column(8)) + across * column(9)
        + beside * (column(10) + own * column(11) + across * column(12))
    ) / beta_sq
    lowest = 0.5 * (alpha + gamma) - jnp.sqrt(0.25 * (alpha - gamma) ** 2 + beta_sq)
    first = gamma - lowest
    united_sq = first * first * size - 2.0 * first * overlap + resid_sq
    factor = math.sqrt(secs * width * width) / jnp.sqrt(jnp.maximum(united_sq, 0.0) + eps)
    back = deltas[pl.ds(sec, 1)][:, 0:1]

    def finish(i, _):
        mine = vec[chunk(i)].astype(jnp.float32)
        ritz = ((image[chunk(i)] + back * mine) * inverse).astype(jnp.bfloat16).astype(jnp.float32)
        ground_ref[chunk(i)] = ((first * mine - beta * ritz) * factor).astype(jnp.bfloat16)
        return 0

    lax.fori_loop(0, CHUNKS, finish, 0)

    def drain(i, _):
        a_copy(0, i, start).wait_send()
        a_copy(1, i, resid).wait_send()
        x_copy(i).wait_send()
        env_copy(i).wait_send()
        return 0

    lax.fori_loop(0, CHUNKS, drain, 0)
    pull_copy(0).wait_send()
    pull_copy(1).wait_send()


def lanczos(table, psi, site, terms, right, secs):
    width = psi.shape[0]
    square = (width, width)
    blocks = lambda *lead: pltpu.VMEM((*lead, *square), jnp.bfloat16)
    wide = pltpu.VMEM(square, jnp.float32)
    sums = pltpu.VMEM((secs, 8, 128), jnp.float32)
    dma = pltpu.SemaphoreType.DMA
    return pl.pallas_call(
        lanczos_kernel,
        out_shape=jax.ShapeDtypeStruct(square, jnp.bfloat16),
        in_specs=[pl.BlockSpec(memory_space=pltpu.SMEM)] + [pl.BlockSpec(memory_space=pl.ANY)] * 4,
        out_specs=pl.BlockSpec(memory_space=pltpu.VMEM),
        scratch_shapes=[
            blocks(), blocks(), blocks(3), blocks(2),
            blocks(), blocks(), blocks(), blocks(), blocks(), blocks(3), blocks(3), blocks(), blocks(),
            blocks(2), blocks(), blocks(), wide, blocks(), blocks(), blocks(),
            pltpu.VMEM((2, *square), jnp.float32), blocks(2), blocks(2),
            sums, sums, pltpu.VMEM((secs, 128), jnp.float32),
            dma((4,)), dma((2, CHUNKS)), dma((2, CHUNKS)), dma((2, CHUNKS)), dma((2, CHUNKS)), dma((CHUNKS,)), dma((CHUNKS,)),
            dma((CHUNKS,)), dma((CHUNKS,)), dma((2,)), dma((2,)), dma((2, secs)), dma((2, secs)),
        ],
        compiler_params=pltpu.CompilerParams(
            collective_id=1, has_side_effects=True, vmem_limit_bytes=62 * 2**20
        ),
        cost_estimate=pl.CostEstimate(flops=16 * 2 * width**3, bytes_accessed=8 * width**2, transcendentals=0),
    )(table, psi, site, terms, right)


def fdot(left, right):
    return jnp.dot(left, right, precision=lax.Precision.HIGHEST, preferred_element_type=jnp.float32)


def spread_lane(tile, lane):
    return jnp.broadcast_to(tile[:, lane : lane + 1], tile.shape)


def spread_row(tile, row):
    return jnp.broadcast_to(tile[row : row + 1, :], tile.shape)


def invert_factor(block, panel):
    size = block.shape[0]
    count = size // 8
    tiles = [block[8 * t : 8 * t + 8] for t in range(count)]
    lane = lax.broadcasted_iota(jnp.int32, (8, size), 1)
    sub = lax.broadcasted_iota(jnp.int32, (8, size), 0)
    scales = [None] * count
    for j in range(0, size, panel):
        top, base = j // 8, j % 8
        cols = [
            {t: spread_lane(tiles[t], j + c) for t in range(top, count)} for c in range(panel)
        ]
        inside = (lane >= j) & (lane < j + panel)
        for t in range(top, count):
            tiles[t] = jnp.where(inside, jnp.where((lane - j == sub + 8 * t - j) , 1.0, 0.0) if t == top else 0.0, tiles[t])
        for c in range(panel):
            row = base + c
            pivot = spread_row(cols[c][top], row)
            inverse = 1.0 / pivot
            scale = lax.rsqrt(pivot)
            scales[top] = scale if scales[top] is None else jnp.where(sub >= row, scale, scales[top])
            below = sub > row
            factor = {}
            for t in range(top, count):
                f = cols[c][t] * inverse
                factor[t] = jnp.where(below, f, 0.0) if t == top else f
            for d in range(c + 1, panel):
                head = spread_row(cols[d][top], row)
                for t in range(top, count):
                    cols[d][t] = cols[d][t] - factor[t] * head
            line = spread_row(tiles[top], row)
            for t in range(top, count):
                tiles[t] = tiles[t] - factor[t] * line
    out = [tiles[t] * scales[t] for t in range(count)]
    full = jnp.concatenate(out, axis=0)
    r = lax.broadcasted_iota(jnp.int32, (size, size), 0)
    q = lax.broadcasted_iota(jnp.int32, (size, size), 1)
    return jnp.where(r >= q, full, 0.0)


def split_dot(left, right):
    result = None
    rest = left
    for _ in range(3):
        part = rest.astype(jnp.bfloat16)
        rest = rest - part.astype(jnp.float32)
        term = dot(part, right)
        result = term if result is None else result + term
    return result


def truncate_kernel(table_ref, ground_ref, cols_ref, kept_ref, dens_ref, basis, basis_t, range_t, gram, inv):
    width, rank = cols_ref.shape
    half = rank // 2
    lane = lax.broadcasted_iota(jnp.int32, (1, rank), 1)
    keep = jnp.where(lane < table_ref[0, 2], 1.0, 0.0)
    for b in range(2):
        block = pl.ds(b * 256, 256)
        rng = (dot(ground_ref[block], cols_ref[...]) * keep).astype(jnp.bfloat16)
        basis[block] = rng
        range_t[:, block] = rng.T
    row = lax.broadcasted_iota(jnp.int32, (rank, rank), 0)
    col = lax.broadcasted_iota(jnp.int32, (rank, rank), 1)
    gram[...] = dot(range_t[...], basis[...]) + jnp.where((row == col) & (col >= table_ref[0, 2]), 1.0, 0.0)
    first = invert_factor(gram[:half, :half], 8)
    upper = fdot(first, gram[:half, half:])
    upper_t = upper.T
    second = invert_factor(gram[half:, half:] - fdot(upper_t, upper), 8)
    inv[:half, :half] = first
    inv[:half, half:] = jnp.zeros((half, half), jnp.float32)
    inv[half:, :half] = -fdot(second, fdot(upper_t, first))
    inv[half:, half:] = second
    basis_t[...] = split_dot(inv[...], range_t[...]).astype(jnp.bfloat16)
    basis[...] = basis_t[...].T
    coeff = dot(basis_t[...], ground_ref[...]).astype(jnp.bfloat16)
    for b in range(2):
        block = pl.ds(b * 256, 256)
        kept_ref[block] = dot(basis[block], coeff).astype(jnp.bfloat16)
    kept_t = kept_ref[...].T
    for b in range(2):
        block = pl.ds(b * 256, 256)
        dens_ref[block] = (dot(kept_ref[block], kept_t) * (1.0 / width)).astype(jnp.bfloat16)


def truncate(table, ground, cols):
    width, rank = cols.shape
    square = jax.ShapeDtypeStruct((width, width), jnp.bfloat16)
    vmem = pl.BlockSpec(memory_space=pltpu.VMEM)
    return pl.pallas_call(
        truncate_kernel,
        out_shape=(square, square),
        in_specs=[pl.BlockSpec(memory_space=pltpu.SMEM), vmem, vmem],
        out_specs=(vmem, vmem),
        scratch_shapes=[
            pltpu.VMEM((width, rank), jnp.bfloat16),
            pltpu.VMEM((rank, width), jnp.bfloat16),
            pltpu.VMEM((rank, width), jnp.bfloat16),
            pltpu.VMEM((rank, rank), jnp.float32),
            pltpu.VMEM((rank, rank), jnp.float32),
        ],
        compiler_params=pltpu.CompilerParams(vmem_limit_bytes=24 * 2**20),
        cost_estimate=pl.CostEstimate(flops=2 * width**3 * 3, bytes_accessed=3 * width**2, transcendentals=0),
    )(table, ground, cols)


def per_device(psi_start, left_site, left_terms, right_terms, start_cols, sector_table):
    ground = lanczos(
        sector_table, psi_start[0, 0], left_site[0, 0], left_terms[0, 0], right_terms[0, 0],
        lax.axis_size("sec"),
    )
    kept, dens = truncate(sector_table, ground, start_cols[0])
    segs = lax.axis_size("seg")
    back = lax.ppermute(dens, "seg", [(i + 1, i) for i in range(segs - 1)])
    return (kept[None, None], back[None, None])


def solution(mesh):
    placed = (
        P("seg", "sec", None, None),
        P("seg", "sec", None, None),
        P("seg", "sec", None, None, None),
        P("seg", "sec", None, None, None),
        P("sec", None, None),
        P("sec", None),
    )
    return jax.shard_map(
        per_device,
        mesh=mesh,
        in_specs=placed,
        out_specs=(P("seg", "sec", None, None), P("seg", "sec", None, None)),
        check_vma=False,
    )
```

```python
import math

import jax
import jax.numpy as jnp
from jax import lax
from jax.experimental import pallas as pl
from jax.experimental.pallas import tpu as pltpu
from jax.sharding import PartitionSpec as P

eps = 1e-06
MESH = pl.DeviceIdType.MESH
CHUNKS = 8
ENV_AT = 1
LEG = 4


def dot(left, right):
    return jnp.dot(left, right, preferred_element_type=jnp.float32)


def dot_left_t(left, right):
    return lax.dot_general(
        left, right, (((0,), (0,)), ((), ())), preferred_element_type=jnp.float32
    )


def dot_right_t(left, right):
    return lax.dot_general(
        left, right, (((1,), (1,)), ((), ())), preferred_element_type=jnp.float32
    )


def total(block):
    return jnp.sum(jnp.sum(block, axis=0, keepdims=True), axis=1, keepdims=True)


def pack(values):
    lane = lax.broadcasted_iota(jnp.int32, (1, 128), 1)
    row = jnp.zeros((1, 128), jnp.float32)
    for k, value in enumerate(values):
        row = jnp.where(lane == k, value, row)
    return row


def fdot(left, right):
    return jnp.dot(left, right, precision=lax.Precision.HIGHEST, preferred_element_type=jnp.float32)


def invert_factor(block, panel):
    size = block.shape[0]
    lane = lax.broadcasted_iota(jnp.int32, (1, size), 1)
    sub = lax.broadcasted_iota(jnp.int32, (8, size), 0)
    done = []
    rest = block
    for j in range(0, size, panel):
        drop = j % 8
        cols = [jnp.broadcast_to(rest[:, j + c : j + c + 1], rest.shape) for c in range(panel)]
        row = lax.broadcasted_iota(jnp.int32, rest.shape, 0)
        inside = (lane >= j) & (lane < j + panel)
        rest = jnp.where(inside, jnp.where(lane - j == row - drop, 1.0, 0.0), rest)
        scales = jnp.ones((8, size), jnp.float32)
        for c in range(panel):
            at = drop + c
            pivot = cols[c][at : at + 1]
            inverse = pl.reciprocal(pivot, approx=True)
            inverse = inverse * (2.0 - pivot * inverse)
            scales = jnp.where(sub == at, lax.rsqrt(pivot), scales)
            factor = jnp.where(row > at, cols[c] * inverse, 0.0)
            for d in range(c + 1, panel):
                cols[d] = cols[d] - factor * cols[d][at : at + 1]
            rest = rest - factor * rest[at : at + 1]
        done.append(rest[:8] * scales)
        rest = rest[8:]
    full = jnp.concatenate(done, axis=0)
    r = lax.broadcasted_iota(jnp.int32, (size, size), 0)
    q = lax.broadcasted_iota(jnp.int32, (size, size), 1)
    return jnp.where(r >= q, full, 0.0)


def split_dot(left, right):
    result = None
    rest = left
    for _ in range(3):
        part = rest.astype(jnp.bfloat16)
        rest = rest - part.astype(jnp.float32)
        term = dot(part, right)
        result = term if result is None else result + term
    return result


def rebuilt(turned, state):
    coeff = dot(turned, state).astype(jnp.bfloat16)
    return dot(turned.T, coeff)


def update_kernel(
    table_ref, psi_hbm, site_hbm, terms_hbm, right_hbm, cols_hbm, kept_ref, dens_ref,
    psi, site, terms, right, cols,
    start, start_z, start_x, site_t, part, built, env, vec, vec_z,
    held, low_z, low_x, image, resid, resid_z, adj, pull, pull_out, pull_in,
    sums1, sums2, deltas,
    ground, ground_n, basis_t, basis_n, range_t, gram, part_n,
    load, a_send, a_recv, z_send, z_recv, x_send, x_recv, env_send, env_recv, pull_send, pull_recv, sum_send, sum_recv, back_send, back_recv,
):
    seg, sec = lax.axis_index("seg"), lax.axis_index("sec")
    segs, secs = lax.axis_size("seg"), lax.axis_size("sec")
    width = psi.shape[0]
    rows = width // CHUNKS
    half = width // 2
    parity = lax.rem(sec, 2)
    partner = sec + 1 - 2 * parity
    relay = lax.rem(sec + 2 - 4 * parity + secs, secs)
    source = lax.rem(sec - 2 + 4 * parity + secs, secs)
    nxt, prv = lax.rem(seg + 1, segs), lax.rem(seg + segs - 1, segs)
    core, z_lo, line = lax.rem(seg, 2), lax.rem(lax.div(seg, 2), 8), lax.div(seg, 16)

    def along_z(distance):
        place = lax.rem(parity * 8 + z_lo + distance, 16)
        return ((line * 8 + lax.rem(place, 8)) * 2 + core, sec - parity + lax.div(place, 8))

    peers = [(seg, lax.rem(sec + d, secs)) for d in range(1, secs)]

    barrier = pltpu.get_barrier_semaphore()
    neighbours = peers + [(nxt, sec), (prv, sec), along_z(LEG), along_z(16 - LEG)]
    for device in neighbours:
        pl.semaphore_signal(barrier, inc=1, device_id=device, device_id_type=MESH)

    loads = [
        pltpu.make_async_copy(psi_hbm, psi, load.at[0]),
        pltpu.make_async_copy(site_hbm, site, load.at[1]),
        pltpu.make_async_copy(terms_hbm, terms, load.at[2]),
        pltpu.make_async_copy(right_hbm, right, load.at[3]),
        pltpu.make_async_copy(cols_hbm, cols, load.at[4]),
    ]
    for copy in loads:
        copy.start()

    def chunk(i):
        return pl.ds(pl.multiple_of(i * rows, rows), rows)

    def halves(b):
        return pl.ds(pl.multiple_of(b * half, half), half)

    def leg(i):
        return along_z(LEG + lax.rem(i, 2) * (16 - 2 * LEG))

    def a_copy(phase, i, block):
        return pltpu.make_async_remote_copy(
            block.at[chunk(i)], (start_z, resid_z)[phase].at[chunk(i)],
            a_send.at[phase, i], a_recv.at[phase, i],
            device_id=(seg, partner), device_id_type=MESH,
        )

    def z_copy(phase, i, target):
        return a_copy(phase, i, (start, resid)[phase])

    def forward(phase, i, block, target):
        return

    def forward_two(phase, j, block, target):
        forward(phase, 2 * j, block, target)
        forward(phase, 2 * j + 1, block, target)

    def x_copy(i):
        return pltpu.make_async_remote_copy(
            start_z.at[chunk(i)], start_x.at[chunk(i)],
            x_send.at[i], x_recv.at[i],
            device_id=(seg, relay), device_id_type=MESH,
        )

    def env_copy(i):
        return pltpu.make_async_remote_copy(
            built.at[:, chunk(i)], env.at[:, chunk(i)], env_send.at[i], env_recv.at[i],
            device_id=(nxt, sec), device_id_type=MESH,
        )

    def pull_copy(k):
        return pltpu.make_async_remote_copy(
            pull_out.at[k], pull_in.at[k], pull_send.at[k], pull_recv.at[k],
            device_id=(seg, source), device_id_type=MESH,
        )

    def back_copy(k, block, target):
        return pltpu.make_async_remote_copy(
            block, target, back_send.at[k], back_recv.at[k], device_id=(prv, sec), device_id_type=MESH
        )

    def sum_copies(phase, buffer):
        return [
            pltpu.make_async_remote_copy(
                buffer.at[sec], buffer.at[sec],
                sum_send.at[phase, d], sum_recv.at[phase, d],
                device_id=peers[d], device_id_type=MESH,
            )
            for d in range(secs - 1)
        ]

    def share(phase, buffer):
        for copy in sum_copies(phase, buffer):
            copy.start()

    def collect(phase, buffer):
        for copy in sum_copies(phase, buffer):
            copy.wait()

    def summed(buffer):
        return jnp.sum(jnp.sum(buffer[...], axis=0), axis=0, keepdims=True)

    live_rows, live_cols = table_ref[0, 0], table_ref[0, 1]

    def mask(first, count):
        i = lax.broadcasted_iota(jnp.int32, (count, width), 0) + first
        j = lax.broadcasted_iota(jnp.int32, (count, width), 1)
        return (i < live_rows) & (j < live_cols)

    zero = jnp.zeros((1, 1), jnp.float32)
    blank = jnp.zeros((8, 128), jnp.float32)
    sums1[sec] = blank
    sums2[sec] = blank
    loads[0].wait()

    def begin(i, norm):
        piece = jnp.where(mask(i * rows, rows), psi[chunk(i)].astype(jnp.float32), 0.0)
        start[chunk(i)] = piece.astype(jnp.bfloat16)
        return norm + total(piece * piece)

    norm = lax.fori_loop(0, CHUNKS, begin, zero)
    sums1[sec, pl.ds(0, 1)] = pack([norm])

    pl.semaphore_wait(barrier, len(neighbours))

    share(0, sums1)

    def send_start(i, _):
        a_copy(0, i, start).start()
        return 0

    lax.fori_loop(0, CHUNKS, send_start, 0)

    loads[1].wait()
    site_t[...] = site[...].T
    loads[2].wait()

    def build(k, _):
        def left(b, _):
            part[halves(b)] = dot(terms[k, halves(b)], site[...]).astype(jnp.bfloat16)
            return 0

        lax.fori_loop(0, 2, left, 0)

        def outer(b, _):
            built[k, halves(b)] = dot(site_t[halves(b)], part[...]).astype(jnp.bfloat16)
            return 0

        lax.fori_loop(0, 2, outer, 0)
        return 0

    lax.fori_loop(0, 3, build, 0)

    loads[3].wait()
    forward_two(0, 0, start, start_z)
    collect(0, sums1)
    scale = 1.0 / jnp.sqrt(summed(sums1)[:, 0:1] + eps)
    has_env = jnp.where(seg > 0, 1.0, 0.0).astype(jnp.float32)
    has_x = jnp.where((sec > 0) & (sec < secs - 1), 1.0, 0.0).astype(jnp.float32)

    def scaled(i, held):
        return (held[chunk(i)].astype(jnp.float32) * scale).astype(jnp.bfloat16)

    def own(i, _):
        vec[chunk(i)] = scaled(i, start)
        return 0

    lax.fori_loop(0, CHUNKS, own, 0)

    right_z, right_x = right.at[1 - parity], right.at[parity]
    env_z, env_x = env.at[2 - parity], env.at[1 + parity]

    def first_z(i):
        z_copy(0, i, start_z).wait_recv()
        x_copy(i).start()
        piece = scaled(i, start_z)
        vec_z[chunk(i)] = piece
        low_z[chunk(i)] = dot(piece, right_z[...]).astype(jnp.bfloat16)

    def first_x(i):
        x_copy(i).wait_recv()
        low_x[chunk(i)] = (dot(scaled(i, start_x), right_x[...]) * has_x).astype(jnp.bfloat16)

    pairs = CHUNKS // 2

    def arrive(j, _):
        forward_two(0, j, start, start_z)
        first_z(2 * j - 2)
        first_z(2 * j - 1)

        @pl.when(j > 1)
        def _():
            first_x(2 * j - 4)
            first_x(2 * j - 3)

        return 0

    def send_env(i, _):
        env_copy(i).start()
        return 0

    def arrive_send(j, _):
        send_env(2 * (j - ENV_AT), 0)
        send_env(2 * (j - ENV_AT) + 1, 0)
        return arrive(j, 0)

    lax.fori_loop(1, ENV_AT, arrive, 0)
    lax.fori_loop(ENV_AT, pairs, arrive_send, 0)
    lax.fori_loop(2 * (pairs - ENV_AT), CHUNKS, send_env, 0)
    first_z(CHUNKS - 2)
    first_z(CHUNKS - 1)
    for i in range(CHUNKS - 4, CHUNKS):
        first_x(i)

    def image_of(i):
        env_copy(i).wait_recv()
        value = dot(env[0, chunk(i)], vec[...])
        value += dot(env_z[chunk(i)], low_z[...])
        value += dot(env_x[chunk(i)], low_x[...])
        return jnp.where(mask(i * rows, rows), value * has_env, 0.0)

    def emit(i, value, guess, sums):
        mine = vec[chunk(i)].astype(jnp.float32)
        piece = value - guess * mine
        image[chunk(i)] = piece
        resid[chunk(i)] = piece.astype(jnp.bfloat16)
        a_copy(1, i, resid).start()
        return sums[0] + total(mine * value), sums[1] + total(mine * mine)

    def quotient(along, size):
        return jnp.where(size > 0.0, along / jnp.where(size > 0.0, size, 1.0), 0.0)

    value = image_of(0)
    mine = vec[chunk(0)].astype(jnp.float32)
    guess = quotient(total(mine * value), total(mine * mine))
    sums = emit(0, value, guess, (zero, zero))

    def apply(i, sums):
        return emit(i, image_of(i), guess, sums)

    sums = lax.fori_loop(1, CHUNKS // 2, apply, sums)
    forward_two(1, 0, resid, resid_z)
    along, size = lax.fori_loop(CHUNKS // 2, CHUNKS, apply, sums)

    def turned(matrix, vector):
        for b in range(2):
            block = slice(b * half, (b + 1) * half)
            adj[block] = dot_left_t(matrix[:, block], vector[...]).astype(jnp.bfloat16)

    def pull_away(k, vector):
        turned(env_x, vector)

        def piece(b, _):
            pull_out[k, halves(b)] = (dot_right_t(adj[halves(b)], right_x[...]) * has_x).astype(jnp.bfloat16)
            return 0

        lax.fori_loop(0, 2, piece, 0)
        pull_copy(k).start()

    def pull_here(k, vector):
        turned(env_z, vector)

        def piece(b, _):
            pull[k, halves(b)] = dot_right_t(adj[halves(b)], right_z[...])
            return 0

        lax.fori_loop(0, 2, piece, 0)

    pull_away(0, resid)
    pull_away(1, vec)
    forward_two(1, 1, resid, resid_z)
    pull_here(0, resid)
    pull_here(1, vec)

    def diagonal(b, sums):
        image_r = dot(env[0, halves(b)], resid[...])
        image_v = dot(env[0, halves(b)], vec[...])
        mine_r, mine_v = resid[halves(b)].astype(jnp.float32), vec[halves(b)].astype(jnp.float32)
        return (
            sums[0] + total(mine_r * image_r),
            sums[1] + total(mine_r * image_v + mine_v * image_r),
            sums[2] + total(mine_v * image_v),
        )

    square_r, mixed, square_v = lax.fori_loop(0, 2, diagonal, (zero, zero, zero))
    ratio = quotient(along, size)

    def norms(i, sums):
        mine = vec[chunk(i)].astype(jnp.float32)
        piece = image[chunk(i)] + (guess - ratio) * mine
        return sums[0] + total(piece * piece), sums[1] + total(mine * piece)

    rho, cross = lax.fori_loop(0, CHUNKS, norms, (zero, zero))
    pull_copy(0).wait_recv()
    pull_copy(1).wait_recv()

    def join(i, sums):
        both = pull[0, chunk(i)] + pull_in[0, chunk(i)].astype(jnp.float32)
        pull[0, chunk(i)] = both
        base = vec_z[chunk(i)].astype(jnp.float32)
        return (
            sums[0] + total(both * base),
            sums[1] + total(pull[1, chunk(i)] * base),
            sums[2] + total(pull_in[1, chunk(i)].astype(jnp.float32) * base),
        )

    base_r, base_v, base_x = lax.fori_loop(0, CHUNKS, join, (zero, zero, zero))

    def meet(i, sums):
        z_copy(1, i, resid_z).wait_recv()
        other = resid_z[chunk(i)].astype(jnp.float32)
        terms = (pull[0, chunk(i)], pull[1, chunk(i)], pull_in[1, chunk(i)].astype(jnp.float32))
        return tuple(old + jnp.sum(term * other, axis=0, keepdims=True) for old, term in zip(sums, terms))

    def meet_two(j, sums):
        forward_two(1, j, resid, resid_z)
        return meet(2 * j - 3, meet(2 * j - 4, sums))

    line_sums = (jnp.zeros((1, width), jnp.float32),) * 3
    line_sums = lax.fori_loop(2, pairs, meet_two, line_sums)
    line_sums = lax.fori_loop(CHUNKS - 4, CHUNKS, meet, line_sums)
    met_r, met_v, met_x = [jnp.sum(line, axis=1, keepdims=True) for line in line_sums]
    sums2[sec, pl.ds(0, 1)] = pack(
        [along, size, rho, cross, ratio, guess]
        + [
            term * has_env
            for term in (square_r + met_r, mixed + met_v, square_v, met_x, base_r, base_v, base_x)
        ]
    )
    share(1, sums2)
    collect(1, sums2)

    gathered = jnp.sum(sums2[...], axis=1)
    column = lambda k: gathered[:, k : k + 1]
    over = lambda value: jnp.sum(value, axis=0, keepdims=True)
    alpha, size = over(column(0)), over(column(1))
    delta = column(4) - alpha
    resid_sq = jnp.maximum(over(column(2) + delta * (2.0 * column(3) + delta * column(1))), 0.0)
    overlap = over(column(3) + delta * column(1))
    beta_sq = resid_sq + eps
    beta = jnp.sqrt(beta_sq)
    inverse = 1.0 / beta
    own = column(5) - alpha
    deltas[...] = jnp.broadcast_to(own, deltas.shape)
    picked = lambda order: jnp.concatenate([deltas[s : s + 1] for s in order], axis=0)[:, 0:1]
    beside = picked([s + 1 - 2 * (s % 2) for s in range(secs)])
    across = picked([(s + 2 - 4 * (s % 2)) % secs for s in range(secs)])
    gamma = over(
        column(6) + own * (column(7) + own * column(8)) + across * column(9)
        + beside * (column(10) + own * column(11) + across * column(12))
    ) / beta_sq
    lowest = 0.5 * (alpha + gamma) - jnp.sqrt(0.25 * (alpha - gamma) ** 2 + beta_sq)
    first = gamma - lowest
    united_sq = first * first * size - 2.0 * first * overlap + resid_sq
    factor = math.sqrt(secs * width * width) / jnp.sqrt(jnp.maximum(united_sq, 0.0) + eps)
    back = deltas[pl.ds(sec, 1)][:, 0:1]

    def finish(i, _):
        mine = vec[chunk(i)].astype(jnp.float32)
        ritz = ((image[chunk(i)] + back * mine) * inverse).astype(jnp.bfloat16).astype(jnp.float32)
        ground[chunk(i)] = ((first * mine - beta * ritz) * factor).astype(jnp.bfloat16)
        return 0

    lax.fori_loop(0, CHUNKS, finish, 0)

    def drain(i, _):
        a_copy(0, i, start).wait_send()
        a_copy(1, i, resid).wait_send()
        x_copy(i).wait_send()
        env_copy(i).wait_send()
        return 0

    lax.fori_loop(0, CHUNKS, drain, 0)
    pull_copy(0).wait_send()
    pull_copy(1).wait_send()

    rank = cols.shape[1]
    near = rank // 2
    low, high = slice(0, near), slice(near, rank)
    ground_back = back_copy(0, ground, ground_n)
    ground_back.start()
    loads[4].wait()
    kept_rank = table_ref[0, 2]
    keep = jnp.where(lax.broadcasted_iota(jnp.int32, (1, rank), 1) < kept_rank, 1.0, 0.0)
    row = lax.broadcasted_iota(jnp.int32, (rank, rank), 0)
    col = lax.broadcasted_iota(jnp.int32, (rank, rank), 1)
    gram[...] = jnp.where((row == col) & (col >= kept_rank), 1.0, 0.0)
    for b in range(2):
        block = slice(b * half, (b + 1) * half)
        ranged = (dot(ground[block], cols[...]) * keep).astype(jnp.bfloat16)
        turned_range = ranged.T
        range_t[:, block] = turned_range
        gram[...] += dot(turned_range, ranged)
    leading = invert_factor(gram[low, low], 8)
    basis_t[low] = split_dot(leading, range_t[low]).astype(jnp.bfloat16)
    backs = [back_copy(1 + b, basis_t.at[block], basis_n.at[block]) for b, block in enumerate((low, high))]
    backs[0].start()
    upper = fdot(leading, gram[low, high])
    upper_t = upper.T
    trailing = invert_factor(gram[high, high] - fdot(upper_t, upper), 8)
    corner = -fdot(trailing, fdot(upper_t, leading))
    basis_t[high] = (split_dot(corner, range_t[low]) + split_dot(trailing, range_t[high])).astype(jnp.bfloat16)
    backs[1].start()

    kept_ref[...] = rebuilt(basis_t[...], ground[...]).astype(jnp.bfloat16)

    ground_back.wait_recv()
    backs[0].wait_recv()
    part_n[...] = rebuilt(basis_n[low], ground_n[...])
    backs[1].wait_recv()
    start[...] = (part_n[...] + rebuilt(basis_n[high], ground_n[...])).astype(jnp.bfloat16)
    has_next = jnp.where(seg < segs - 1, 1.0 / width, 0.0).astype(jnp.float32)

    def density(b, _):
        dens_ref[halves(b)] = (dot_right_t(start[halves(b)], start[...]) * has_next).astype(jnp.bfloat16)
        return 0

    lax.fori_loop(0, 2, density, 0)
    ground_back.wait_send()
    for copy in backs:
        copy.wait_send()


def update(table, psi, site, terms, right, cols, secs):
    width = psi.shape[0]
    rank = cols.shape[1]
    square = (width, width)
    tall = pltpu.VMEM((rank, width), jnp.bfloat16)
    blocks = lambda *lead: pltpu.VMEM((*lead, *square), jnp.bfloat16)
    wide = pltpu.VMEM(square, jnp.float32)
    sums = pltpu.VMEM((secs, 8, 128), jnp.float32)
    dma = pltpu.SemaphoreType.DMA
    return pl.pallas_call(
        update_kernel,
        out_shape=(jax.ShapeDtypeStruct(square, jnp.bfloat16),) * 2,
        in_specs=[pl.BlockSpec(memory_space=pltpu.SMEM)] + [pl.BlockSpec(memory_space=pl.ANY)] * 5,
        out_specs=(pl.BlockSpec(memory_space=pltpu.VMEM),) * 2,
        scratch_shapes=[
            blocks(), blocks(), blocks(3), blocks(2), pltpu.VMEM((width, rank), jnp.bfloat16),
            blocks(), blocks(), blocks(), blocks(), blocks(), blocks(3), blocks(3), blocks(), blocks(),
            blocks(2), blocks(), blocks(), wide, blocks(), blocks(), blocks(),
            pltpu.VMEM((2, *square), jnp.float32), blocks(2), blocks(2),
            sums, sums, pltpu.VMEM((secs, 128), jnp.float32),
            blocks(), blocks(), tall, tall, tall, pltpu.VMEM((rank, rank), jnp.float32), wide,
            dma((5,)), dma((2, CHUNKS)), dma((2, CHUNKS)), dma((2, CHUNKS)), dma((2, CHUNKS)), dma((CHUNKS,)), dma((CHUNKS,)),
            dma((CHUNKS,)), dma((CHUNKS,)), dma((2,)), dma((2,)), dma((2, secs)), dma((2, secs)), dma((3,)), dma((3,)),
        ],
        compiler_params=pltpu.CompilerParams(
            collective_id=1, has_side_effects=True, vmem_limit_bytes=62 * 2**20
        ),
        cost_estimate=pl.CostEstimate(flops=16 * 2 * width**3, bytes_accessed=8 * width**2, transcendentals=0),
    )(table, psi, site, terms, right, cols)


def per_device(psi_start, left_site, left_terms, right_terms, start_cols, sector_table):
    kept, back = update(
        sector_table, psi_start[0, 0], left_site[0, 0], left_terms[0, 0], right_terms[0, 0],
        start_cols[0], lax.axis_size("sec"),
    )
    return (kept[None, None], back[None, None])


def solution(mesh):
    placed = (
        P("seg", "sec", None, None),
        P("seg", "sec", None, None),
        P("seg", "sec", None, None, None),
        P("seg", "sec", None, None, None),
        P("sec", None, None),
        P("sec", None),
    )
    return jax.shard_map(
        per_device,
        mesh=mesh,
        in_specs=placed,
        out_specs=(P("seg", "sec", None, None), P("seg", "sec", None, None)),
        check_vma=False,
    )
```

```python
import math

import jax
import jax.numpy as jnp
from jax import lax
from jax.experimental import pallas as pl
from jax.experimental.pallas import tpu as pltpu
from jax.sharding import PartitionSpec as P

eps = 1e-06
MESH = pl.DeviceIdType.MESH
CHUNKS = 8
ENV_AT = 1


def dot(left, right):
    return jnp.dot(left, right, preferred_element_type=jnp.float32)


def dot_left_t(left, right):
    return lax.dot_general(
        left, right, (((0,), (0,)), ((), ())), preferred_element_type=jnp.float32
    )


def dot_right_t(left, right):
    return lax.dot_general(
        left, right, (((1,), (1,)), ((), ())), preferred_element_type=jnp.float32
    )


def total(block):
    return jnp.sum(jnp.sum(block, axis=0, keepdims=True), axis=1, keepdims=True)


def pack(values):
    lane = lax.broadcasted_iota(jnp.int32, (1, 128), 1)
    row = jnp.zeros((1, 128), jnp.float32)
    for k, value in enumerate(values):
        row = jnp.where(lane == k, value, row)
    return row


def fdot(left, right):
    return jnp.dot(left, right, precision=lax.Precision.HIGHEST, preferred_element_type=jnp.float32)


def invert_factor(block, panel):
    size = block.shape[0]
    lane = lax.broadcasted_iota(jnp.int32, (1, size), 1)
    sub = lax.broadcasted_iota(jnp.int32, (8, size), 0)
    done = []
    rest = block
    for j in range(0, size, panel):
        drop = j % 8
        cols = [jnp.broadcast_to(rest[:, j + c : j + c + 1], rest.shape) for c in range(panel)]
        row = lax.broadcasted_iota(jnp.int32, rest.shape, 0)
        inside = (lane >= j) & (lane < j + panel)
        rest = jnp.where(inside, jnp.where(lane - j == row - drop, 1.0, 0.0), rest)
        scales = jnp.ones((8, size), jnp.float32)
        for c in range(panel):
            at = drop + c
            pivot = cols[c][at : at + 1]
            inverse = pl.reciprocal(pivot, approx=True)
            inverse = inverse * (2.0 - pivot * inverse)
            scales = jnp.where(sub == at, lax.rsqrt(pivot), scales)
            factor = jnp.where(row > at, cols[c] * inverse, 0.0)
            for d in range(c + 1, panel):
                cols[d] = cols[d] - factor * cols[d][at : at + 1]
            rest = rest - factor * rest[at : at + 1]
        done.append(rest[:8] * scales)
        rest = rest[8:]
    full = jnp.concatenate(done, axis=0)
    r = lax.broadcasted_iota(jnp.int32, (size, size), 0)
    q = lax.broadcasted_iota(jnp.int32, (size, size), 1)
    return jnp.where(r >= q, full, 0.0)


def split_dot(left, right):
    result = None
    rest = left
    for _ in range(3):
        part = rest.astype(jnp.bfloat16)
        rest = rest - part.astype(jnp.float32)
        term = dot(part, right)
        result = term if result is None else result + term
    return result


def rebuilt(turned, state):
    coeff = dot(turned, state).astype(jnp.bfloat16)
    return dot(turned.T, coeff)


def update_kernel(
    table_ref, psi_hbm, site_hbm, terms_hbm, right_hbm, cols_hbm, kept_ref, dens_ref,
    psi, site, terms, right, cols,
    start, start_z, start_x, site_t, part, built, env, vec, vec_z,
    low_z, low_x, image, resid, resid_z, adj, pull, pull_out, pull_in,
    sums1, sums2, deltas,
    ground, ground_n, basis_t, basis_n, range_t, gram, part_n,
    load, z_send, z_recv, x_send, x_recv, env_send, env_recv, pull_send, pull_recv, sum_send, sum_recv, back_send, back_recv,
):
    seg, sec = lax.axis_index("seg"), lax.axis_index("sec")
    segs, secs = lax.axis_size("seg"), lax.axis_size("sec")
    width = psi.shape[0]
    rows = width // CHUNKS
    half = width // 2
    parity = lax.rem(sec, 2)
    partner = sec + 1 - 2 * parity
    relay = lax.rem(sec + 2 - 4 * parity + secs, secs)
    source = lax.rem(sec - 2 + 4 * parity + secs, secs)
    nxt, prv = lax.rem(seg + 1, segs), lax.rem(seg + segs - 1, segs)
    peers = [(seg, lax.rem(sec + d, secs)) for d in range(1, secs)]

    barrier = pltpu.get_barrier_semaphore()
    neighbours = peers + [(nxt, sec), (prv, sec)]
    for device in neighbours:
        pl.semaphore_signal(barrier, inc=1, device_id=device, device_id_type=MESH)

    loads = [
        pltpu.make_async_copy(psi_hbm, psi, load.at[0]),
        pltpu.make_async_copy(site_hbm, site, load.at[1]),
        pltpu.make_async_copy(terms_hbm, terms, load.at[2]),
        pltpu.make_async_copy(right_hbm, right, load.at[3]),
        pltpu.make_async_copy(cols_hbm, cols, load.at[4]),
    ]
    for copy in loads:
        copy.start()

    def chunk(i):
        return pl.ds(pl.multiple_of(i * rows, rows), rows)

    def halves(b):
        return pl.ds(pl.multiple_of(b * half, half), half)

    def z_copy(phase, i):
        block, target = ((start, start_z), (resid, resid_z))[phase]
        return pltpu.make_async_remote_copy(
            block.at[chunk(i)], target.at[chunk(i)],
            z_send.at[phase, i], z_recv.at[phase, i],
            device_id=(seg, partner), device_id_type=MESH,
        )

    def x_copy(i):
        return pltpu.make_async_remote_copy(
            start_z.at[chunk(i)], start_x.at[chunk(i)],
            x_send.at[i], x_recv.at[i],
            device_id=(seg, relay), device_id_type=MESH,
        )

    def env_copy(i):
        return pltpu.make_async_remote_copy(
            built.at[:, chunk(i)], env.at[:, chunk(i)], env_send.at[i], env_recv.at[i],
            device_id=(nxt, sec), device_id_type=MESH,
        )

    def pull_copy(k):
        return pltpu.make_async_remote_copy(
            pull_out.at[k], pull_in.at[k], pull_send.at[k], pull_recv.at[k],
            device_id=(seg, source), device_id_type=MESH,
        )

    def back_copy(k, block, target):
        return pltpu.make_async_remote_copy(
            block, target, back_send.at[k], back_recv.at[k], device_id=(prv, sec), device_id_type=MESH
        )

    def sum_copies(phase, buffer):
        return [
            pltpu.make_async_remote_copy(
                buffer.at[pl.ds(sec, 1)], buffer.at[pl.ds(sec, 1)],
                sum_send.at[phase, d], sum_recv.at[phase, d],
                device_id=peers[d], device_id_type=MESH,
            )
            for d in range(secs - 1)
        ]

    def share(phase, buffer):
        for copy in sum_copies(phase, buffer):
            copy.start()

    def collect(phase, buffer):
        for copy in sum_copies(phase, buffer):
            copy.wait()

    def summed(buffer):
        return jnp.sum(buffer[...], axis=0, keepdims=True)

    live_rows, live_cols = table_ref[0, 0], table_ref[0, 1]

    def mask(first, count):
        i = lax.broadcasted_iota(jnp.int32, (count, width), 0) + first
        j = lax.broadcasted_iota(jnp.int32, (count, width), 1)
        return (i < live_rows) & (j < live_cols)

    zero = jnp.zeros((1, 1), jnp.float32)
    loads[0].wait()

    def begin(i, norm):
        piece = jnp.where(mask(i * rows, rows), psi[chunk(i)].astype(jnp.float32), 0.0)
        start[chunk(i)] = piece.astype(jnp.bfloat16)
        return norm + total(piece * piece)

    norm = begin(0, zero)
    pl.semaphore_wait(barrier, len(neighbours))
    z_copy(0, 0).start()
    norm = lax.fori_loop(1, CHUNKS, begin, norm)
    sums1[pl.ds(sec, 1)] = pack([norm])
    share(0, sums1)

    def send_start(i, _):
        z_copy(0, i).start()
        return 0

    lax.fori_loop(1, CHUNKS, send_start, 0)

    loads[1].wait()
    site_t[...] = site[...].T
    loads[2].wait()

    def build(k, _):
        def left(b, _):
            part[halves(b)] = dot(terms[k, halves(b)], site[...]).astype(jnp.bfloat16)
            return 0

        lax.fori_loop(0, 2, left, 0)

        def outer(b, _):
            built[k, halves(b)] = dot(site_t[halves(b)], part[...]).astype(jnp.bfloat16)
            return 0

        lax.fori_loop(0, 2, outer, 0)
        return 0

    lax.fori_loop(0, 3, build, 0)

    loads[3].wait()
    collect(0, sums1)
    scale = 1.0 / jnp.sqrt(summed(sums1)[:, 0:1] + eps)
    has_env = jnp.where(seg > 0, 1.0, 0.0).astype(jnp.float32)
    has_x = jnp.where((sec > 0) & (sec < secs - 1), 1.0, 0.0).astype(jnp.float32)

    def scaled(i, held):
        return (held[chunk(i)].astype(jnp.float32) * scale).astype(jnp.bfloat16)

    def own(i, _):
        vec[chunk(i)] = scaled(i, start)
        return 0

    lax.fori_loop(0, CHUNKS, own, 0)

    right_z, right_x = right.at[1 - parity], right.at[parity]
    env_z, env_x = env.at[2 - parity], env.at[1 + parity]

    def first_z(i):
        z_copy(0, i).wait_recv()
        x_copy(i).start()
        piece = scaled(i, start_z)
        vec_z[chunk(i)] = piece
        low_z[chunk(i)] = dot(piece, right_z[...]).astype(jnp.bfloat16)

    def first_x(i):
        x_copy(i).wait_recv()
        low_x[chunk(i)] = (dot(scaled(i, start_x), right_x[...]) * has_x).astype(jnp.bfloat16)

    pairs = CHUNKS // 2

    def arrive(j, _):
        first_z(2 * j - 2)
        first_z(2 * j - 1)

        @pl.when(j > 1)
        def _():
            first_x(2 * j - 4)
            first_x(2 * j - 3)

        return 0

    def send_env(i, _):
        env_copy(i).start()
        return 0

    def arrive_send(j, _):
        send_env(2 * (j - ENV_AT), 0)
        send_env(2 * (j - ENV_AT) + 1, 0)
        return arrive(j, 0)

    lax.fori_loop(1, ENV_AT, arrive, 0)
    lax.fori_loop(ENV_AT, pairs, arrive_send, 0)
    lax.fori_loop(2 * (pairs - ENV_AT), CHUNKS, send_env, 0)
    first_z(CHUNKS - 2)
    first_z(CHUNKS - 1)
    for i in range(CHUNKS - 4, CHUNKS):
        first_x(i)

    def image_of(i):
        env_copy(i).wait_recv()
        value = dot(env[0, chunk(i)], vec[...])
        value += dot(env_z[chunk(i)], low_z[...])
        value += dot(env_x[chunk(i)], low_x[...])
        return jnp.where(mask(i * rows, rows), value * has_env, 0.0)

    def emit(i, value, guess, sums):
        mine = vec[chunk(i)].astype(jnp.float32)
        piece = value - guess * mine
        image[chunk(i)] = piece
        resid[chunk(i)] = piece.astype(jnp.bfloat16)
        z_copy(1, i).start()
        return sums[0] + total(mine * value), sums[1] + total(mine * mine)

    def quotient(along, size):
        return jnp.where(size > 0.0, along / jnp.where(size > 0.0, size, 1.0), 0.0)

    value = image_of(0)
    mine = vec[chunk(0)].astype(jnp.float32)
    guess = quotient(total(mine * value), total(mine * mine))
    sums = emit(0, value, guess, (zero, zero))

    def apply(i, sums):
        return emit(i, image_of(i), guess, sums)

    along, size = lax.fori_loop(1, CHUNKS, apply, sums)

    def turned(matrix, vector):
        for b in range(2):
            block = slice(b * half, (b + 1) * half)
            adj[block] = dot_left_t(matrix[:, block], vector[...]).astype(jnp.bfloat16)

    def pull_away(k, vector):
        turned(env_x, vector)

        def piece(b, _):
            pull_out[k, halves(b)] = (dot_right_t(adj[halves(b)], right_x[...]) * has_x).astype(jnp.bfloat16)
            return 0

        lax.fori_loop(0, 2, piece, 0)
        pull_copy(k).start()

    def pull_here(k, vector):
        turned(env_z, vector)

        def piece(b, _):
            pull[k, halves(b)] = dot_right_t(adj[halves(b)], right_z[...])
            return 0

        lax.fori_loop(0, 2, piece, 0)

    pull_away(0, resid)
    pull_away(1, vec)
    pull_here(0, resid)
    pull_here(1, vec)

    def diagonal(b, sums):
        image_r = dot(env[0, halves(b)], resid[...])
        image_v = dot(env[0, halves(b)], vec[...])
        mine_r, mine_v = resid[halves(b)].astype(jnp.float32), vec[halves(b)].astype(jnp.float32)
        return (
            sums[0] + total(mine_r * image_r),
            sums[1] + total(mine_r * image_v + mine_v * image_r),
            sums[2] + total(mine_v * image_v),
        )

    square_r, mixed, square_v = lax.fori_loop(0, 2, diagonal, (zero, zero, zero))
    ratio = quotient(along, size)

    def norms(i, sums):
        mine = vec[chunk(i)].astype(jnp.float32)
        piece = image[chunk(i)] + (guess - ratio) * mine
        return sums[0] + total(piece * piece), sums[1] + total(mine * piece)

    rho, cross = lax.fori_loop(0, CHUNKS, norms, (zero, zero))
    pull_copy(0).wait_recv()
    pull_copy(1).wait_recv()

    def join(i, sums):
        both = pull[0, chunk(i)] + pull_in[0, chunk(i)].astype(jnp.float32)
        pull[0, chunk(i)] = both
        base = vec_z[chunk(i)].astype(jnp.float32)
        return (
            sums[0] + total(both * base),
            sums[1] + total(pull[1, chunk(i)] * base),
            sums[2] + total(pull_in[1, chunk(i)].astype(jnp.float32) * base),
        )

    base_r, base_v, base_x = lax.fori_loop(0, CHUNKS, join, (zero, zero, zero))

    def meet(i, sums):
        z_copy(1, i).wait_recv()
        other = resid_z[chunk(i)].astype(jnp.float32)
        terms = (pull[0, chunk(i)], pull[1, chunk(i)], pull_in[1, chunk(i)].astype(jnp.float32))
        return tuple(old + jnp.sum(term * other, axis=0, keepdims=True) for old, term in zip(sums, terms))

    line_sums = lax.fori_loop(0, CHUNKS, meet, (jnp.zeros((1, width), jnp.float32),) * 3)
    met_r, met_v, met_x = [jnp.sum(line, axis=1, keepdims=True) for line in line_sums]
    sums2[pl.ds(sec, 1)] = pack(
        [along, size, rho, cross, ratio, guess]
        + [
            term * has_env
            for term in (square_r + met_r, mixed + met_v, square_v, met_x, base_r, base_v, base_x)
        ]
    )
    share(1, sums2)
    collect(1, sums2)

    gathered = sums2[...]
    column = lambda k: gathered[:, k : k + 1]
    over = lambda value: jnp.sum(value, axis=0, keepdims=True)
    alpha, size = over(column(0)), over(column(1))
    delta = column(4) - alpha
    resid_sq = jnp.maximum(over(column(2) + delta * (2.0 * column(3) + delta * column(1))), 0.0)
    overlap = over(column(3) + delta * column(1))
    beta_sq = resid_sq + eps
    beta = jnp.sqrt(beta_sq)
    inverse = 1.0 / beta
    own = column(5) - alpha
    deltas[...] = jnp.broadcast_to(own, deltas.shape)
    picked = lambda order: jnp.concatenate([deltas[s : s + 1] for s in order], axis=0)[:, 0:1]
    beside = picked([s + 1 - 2 * (s % 2) for s in range(secs)])
    across = picked([(s + 2 - 4 * (s % 2)) % secs for s in range(secs)])
    gamma = over(
        column(6) + own * (column(7) + own * column(8)) + across * column(9)
        + beside * (column(10) + own * column(11) + across * column(12))
    ) / beta_sq
    lowest = 0.5 * (alpha + gamma) - jnp.sqrt(0.25 * (alpha - gamma) ** 2 + beta_sq)
    first = gamma - lowest
    united_sq = first * first * size - 2.0 * first * overlap + resid_sq
    factor = math.sqrt(secs * width * width) / jnp.sqrt(jnp.maximum(united_sq, 0.0) + eps)
    back = deltas[pl.ds(sec, 1)][:, 0:1]

    def finish(i, _):
        mine = vec[chunk(i)].astype(jnp.float32)
        ritz = ((image[chunk(i)] + back * mine) * inverse).astype(jnp.bfloat16).astype(jnp.float32)
        ground[chunk(i)] = ((first * mine - beta * ritz) * factor).astype(jnp.bfloat16)
        return 0

    lax.fori_loop(0, CHUNKS, finish, 0)

    def drain(i, _):
        z_copy(0, i).wait_send()
        z_copy(1, i).wait_send()
        x_copy(i).wait_send()
        env_copy(i).wait_send()
        return 0

    lax.fori_loop(0, CHUNKS, drain, 0)
    pull_copy(0).wait_send()
    pull_copy(1).wait_send()

    rank = cols.shape[1]
    near = rank // 2
    low, high = slice(0, near), slice(near, rank)
    ground_back = back_copy(0, ground, ground_n)
    ground_back.start()
    loads[4].wait()
    kept_rank = table_ref[0, 2]
    keep = jnp.where(lax.broadcasted_iota(jnp.int32, (1, rank), 1) < kept_rank, 1.0, 0.0)
    row = lax.broadcasted_iota(jnp.int32, (rank, rank), 0)
    col = lax.broadcasted_iota(jnp.int32, (rank, rank), 1)
    gram[...] = jnp.where((row == col) & (col >= kept_rank), 1.0, 0.0)
    for b in range(2):
        block = slice(b * half, (b + 1) * half)
        ranged = (dot(ground[block], cols[...]) * keep).astype(jnp.bfloat16)
        turned_range = ranged.T
        range_t[:, block] = turned_range
        gram[...] += dot(turned_range, ranged)
    leading = invert_factor(gram[low, low], 8)
    basis_t[low] = split_dot(leading, range_t[low]).astype(jnp.bfloat16)
    backs = [back_copy(1 + b, basis_t.at[block], basis_n.at[block]) for b, block in enumerate((low, high))]
    backs[0].start()
    upper = fdot(leading, gram[low, high])
    upper_t = upper.T
    trailing = invert_factor(gram[high, high] - fdot(upper_t, upper), 8)
    corner = -fdot(trailing, fdot(upper_t, leading))
    basis_t[high] = (split_dot(corner, range_t[low]) + split_dot(trailing, range_t[high])).astype(jnp.bfloat16)
    backs[1].start()

    kept_ref[...] = rebuilt(basis_t[...], ground[...]).astype(jnp.bfloat16)

    ground_back.wait_recv()
    backs[0].wait_recv()
    part_n[...] = rebuilt(basis_n[low], ground_n[...])
    backs[1].wait_recv()
    start[...] = (part_n[...] + rebuilt(basis_n[high], ground_n[...])).astype(jnp.bfloat16)
    has_next = jnp.where(seg < segs - 1, 1.0 / width, 0.0).astype(jnp.float32)

    def density(b, _):
        dens_ref[halves(b)] = (dot_right_t(start[halves(b)], start[...]) * has_next).astype(jnp.bfloat16)
        return 0

    lax.fori_loop(0, 2, density, 0)
    ground_back.wait_send()
    for copy in backs:
        copy.wait_send()


def update(table, psi, site, terms, right, cols, secs):
    width = psi.shape[0]
    rank = cols.shape[1]
    square = (width, width)
    tall = pltpu.VMEM((rank, width), jnp.bfloat16)
    blocks = lambda *lead: pltpu.VMEM((*lead, *square), jnp.bfloat16)
    wide = pltpu.VMEM(square, jnp.float32)
    sums = pltpu.VMEM((secs, 128), jnp.float32)
    dma = pltpu.SemaphoreType.DMA
    return pl.pallas_call(
        update_kernel,
        out_shape=(jax.ShapeDtypeStruct(square, jnp.bfloat16),) * 2,
        in_specs=[pl.BlockSpec(memory_space=pltpu.SMEM)] + [pl.BlockSpec(memory_space=pl.ANY)] * 5,
        out_specs=(pl.BlockSpec(memory_space=pltpu.VMEM),) * 2,
        scratch_shapes=[
            blocks(), blocks(), blocks(3), blocks(2), pltpu.VMEM((width, rank), jnp.bfloat16),
            blocks(), blocks(), blocks(), blocks(), blocks(), blocks(3), blocks(3), blocks(), blocks(),
            blocks(), blocks(), wide, blocks(), blocks(), blocks(),
            pltpu.VMEM((2, *square), jnp.float32), blocks(2), blocks(2),
            sums, sums, pltpu.VMEM((secs, 128), jnp.float32),
            blocks(), blocks(), tall, tall, tall, pltpu.VMEM((rank, rank), jnp.float32), wide,
            dma((5,)), dma((2, CHUNKS)), dma((2, CHUNKS)), dma((CHUNKS,)), dma((CHUNKS,)),
            dma((CHUNKS,)), dma((CHUNKS,)), dma((2,)), dma((2,)), dma((2, secs)), dma((2, secs)), dma((3,)), dma((3,)),
        ],
        compiler_params=pltpu.CompilerParams(
            collective_id=1, has_side_effects=True, vmem_limit_bytes=62 * 2**20
        ),
        cost_estimate=pl.CostEstimate(flops=16 * 2 * width**3, bytes_accessed=8 * width**2, transcendentals=0),
    )(table, psi, site, terms, right, cols)


def per_device(psi_start, left_site, left_terms, right_terms, start_cols, sector_table):
    kept, back = update(
        sector_table, psi_start[0, 0], left_site[0, 0], left_terms[0, 0], right_terms[0, 0],
        start_cols[0], lax.axis_size("sec"),
    )
    return (kept[None, None], back[None, None])


def solution(mesh):
    placed = (
        P("seg", "sec", None, None),
        P("seg", "sec", None, None),
        P("seg", "sec", None, None, None),
        P("seg", "sec", None, None, None),
        P("sec", None, None),
        P("sec", None),
    )
    return jax.shard_map(
        per_device,
        mesh=mesh,
        in_specs=placed,
        out_specs=(P("seg", "sec", None, None), P("seg", "sec", None, None)),
        check_vma=False,
    )
```

```python
import math

import jax
import jax.numpy as jnp
from jax import lax
from jax.experimental import pallas as pl
from jax.experimental.pallas import tpu as pltpu
from jax.sharding import PartitionSpec as P

eps = 1e-06
MESH = pl.DeviceIdType.MESH
CHUNKS = 8
ENV_AT = 1


def dot(left, right):
    return jnp.dot(left, right, preferred_element_type=jnp.float32)


def dot_left_t(left, right):
    return lax.dot_general(
        left, right, (((0,), (0,)), ((), ())), preferred_element_type=jnp.float32
    )


def dot_right_t(left, right):
    return lax.dot_general(
        left, right, (((1,), (1,)), ((), ())), preferred_element_type=jnp.float32
    )


def total(block):
    return jnp.sum(jnp.sum(block, axis=0, keepdims=True), axis=1, keepdims=True)


def pack(values):
    lane = lax.broadcasted_iota(jnp.int32, (1, 128), 1)
    row = jnp.zeros((1, 128), jnp.float32)
    for k, value in enumerate(values):
        row = jnp.where(lane == k, value, row)
    return row


def fdot(left, right):
    return jnp.dot(left, right, precision=lax.Precision.HIGHEST, preferred_element_type=jnp.float32)


def invert_factor(block, panel):
    size = block.shape[0]
    lane = lax.broadcasted_iota(jnp.int32, (1, size), 1)
    sub = lax.broadcasted_iota(jnp.int32, (8, size), 0)
    done = []
    rest = block
    for j in range(0, size, panel):
        drop = j % 8
        cols = [jnp.broadcast_to(rest[:, j + c : j + c + 1], rest.shape) for c in range(panel)]
        row = lax.broadcasted_iota(jnp.int32, rest.shape, 0)
        inside = (lane >= j) & (lane < j + panel)
        rest = jnp.where(inside, jnp.where(lane - j == row - drop, 1.0, 0.0), rest)
        scales = jnp.ones((8, size), jnp.float32)
        for c in range(panel):
            at = drop + c
            pivot = cols[c][at : at + 1]
            inverse = pl.reciprocal(pivot, approx=True)
            inverse = inverse * (2.0 - pivot * inverse)
            scales = jnp.where(sub == at, lax.rsqrt(pivot), scales)
            factor = jnp.where(row > at, cols[c] * inverse, 0.0)
            for d in range(c + 1, panel):
                cols[d] = cols[d] - factor * cols[d][at : at + 1]
            rest = rest - factor * rest[at : at + 1]
        done.append(rest[:8] * scales)
        rest = rest[8:]
    full = jnp.concatenate(done, axis=0)
    r = lax.broadcasted_iota(jnp.int32, (size, size), 0)
    q = lax.broadcasted_iota(jnp.int32, (size, size), 1)
    return jnp.where(r >= q, full, 0.0)


def split_dot(left, right):
    result = None
    rest = left
    for _ in range(3):
        part = rest.astype(jnp.bfloat16)
        rest = rest - part.astype(jnp.float32)
        term = dot(part, right)
        result = term if result is None else result + term
    return result


def rebuilt(turned, state):
    coeff = dot(turned, state).astype(jnp.bfloat16)
    return dot(turned.T, coeff)


def update_kernel(
    table_ref, psi_hbm, site_hbm, terms_hbm, right_hbm, cols_hbm, kept_ref, next_ref,
    psi, site, terms, right, cols,
    start, start_z, start_x, site_t, part, built, env, vec, vec_z,
    low_z, low_x, image, resid, resid_z, adj, pull, pull_out, pull_in,
    sums1, sums2, deltas,
    ground, ground_n, basis_t, basis_n, range_t, gram, part_n,
    load, z_send, z_recv, x_send, x_recv, env_send, env_recv, pull_send, pull_recv, sum_send, sum_recv, back_send, back_recv,
):
    seg, sec = lax.axis_index("seg"), lax.axis_index("sec")
    segs, secs = lax.axis_size("seg"), lax.axis_size("sec")
    width = psi.shape[0]
    rows = width // CHUNKS
    half = width // 2
    parity = lax.rem(sec, 2)
    partner = sec + 1 - 2 * parity
    relay = lax.rem(sec + 2 - 4 * parity + secs, secs)
    source = lax.rem(sec - 2 + 4 * parity + secs, secs)
    nxt, prv = lax.rem(seg + 1, segs), lax.rem(seg + segs - 1, segs)
    peers = [(seg, lax.rem(sec + d, secs)) for d in range(1, secs)]

    barrier = pltpu.get_barrier_semaphore()
    neighbours = peers + [(nxt, sec), (prv, sec)]
    for device in neighbours:
        pl.semaphore_signal(barrier, inc=1, device_id=device, device_id_type=MESH)

    loads = [
        pltpu.make_async_copy(psi_hbm, psi, load.at[0]),
        pltpu.make_async_copy(site_hbm, site, load.at[1]),
        pltpu.make_async_copy(terms_hbm, terms, load.at[2]),
        pltpu.make_async_copy(right_hbm, right, load.at[3]),
        pltpu.make_async_copy(cols_hbm, cols, load.at[4]),
    ]
    for copy in loads:
        copy.start()

    def chunk(i):
        return pl.ds(pl.multiple_of(i * rows, rows), rows)

    def halves(b):
        return pl.ds(pl.multiple_of(b * half, half), half)

    def z_copy(phase, i):
        block, target = ((start, start_z), (resid, resid_z))[phase]
        return pltpu.make_async_remote_copy(
            block.at[chunk(i)], target.at[chunk(i)],
            z_send.at[phase, i], z_recv.at[phase, i],
            device_id=(seg, partner), device_id_type=MESH,
        )

    def x_copy(i):
        return pltpu.make_async_remote_copy(
            start_z.at[chunk(i)], start_x.at[chunk(i)],
            x_send.at[i], x_recv.at[i],
            device_id=(seg, relay), device_id_type=MESH,
        )

    def env_copy(i):
        return pltpu.make_async_remote_copy(
            built.at[:, chunk(i)], env.at[:, chunk(i)], env_send.at[i], env_recv.at[i],
            device_id=(nxt, sec), device_id_type=MESH,
        )

    def pull_copy(k):
        return pltpu.make_async_remote_copy(
            pull_out.at[k], pull_in.at[k], pull_send.at[k], pull_recv.at[k],
            device_id=(seg, source), device_id_type=MESH,
        )

    def back_copy(k, block, target):
        return pltpu.make_async_remote_copy(
            block, target, back_send.at[k], back_recv.at[k], device_id=(prv, sec), device_id_type=MESH
        )

    def sum_copies(phase, buffer):
        return [
            pltpu.make_async_remote_copy(
                buffer.at[pl.ds(sec, 1)], buffer.at[pl.ds(sec, 1)],
                sum_send.at[phase, d], sum_recv.at[phase, d],
                device_id=peers[d], device_id_type=MESH,
            )
            for d in range(secs - 1)
        ]

    def share(phase, buffer):
        for copy in sum_copies(phase, buffer):
            copy.start()

    def collect(phase, buffer):
        for copy in sum_copies(phase, buffer):
            copy.wait()

    def summed(buffer):
        return jnp.sum(buffer[...], axis=0, keepdims=True)

    live_rows, live_cols = table_ref[0, 0], table_ref[0, 1]

    def mask(first, count):
        i = lax.broadcasted_iota(jnp.int32, (count, width), 0) + first
        j = lax.broadcasted_iota(jnp.int32, (count, width), 1)
        return (i < live_rows) & (j < live_cols)

    zero = jnp.zeros((1, 1), jnp.float32)
    loads[0].wait()

    def begin(i, norm):
        piece = jnp.where(mask(i * rows, rows), psi[chunk(i)].astype(jnp.float32), 0.0)
        start[chunk(i)] = piece.astype(jnp.bfloat16)
        return norm + total(piece * piece)

    norm = begin(0, zero)
    pl.semaphore_wait(barrier, len(neighbours))
    z_copy(0, 0).start()
    norm = lax.fori_loop(1, CHUNKS, begin, norm)
    sums1[pl.ds(sec, 1)] = pack([norm])
    share(0, sums1)

    def send_start(i, _):
        z_copy(0, i).start()
        return 0

    lax.fori_loop(1, CHUNKS, send_start, 0)

    loads[1].wait()
    site_t[...] = site[...].T
    loads[2].wait()

    def build(k, _):
        def left(b, _):
            part[halves(b)] = dot(terms[k, halves(b)], site[...]).astype(jnp.bfloat16)
            return 0

        lax.fori_loop(0, 2, left, 0)

        def outer(b, _):
            built[k, halves(b)] = dot(site_t[halves(b)], part[...]).astype(jnp.bfloat16)
            return 0

        lax.fori_loop(0, 2, outer, 0)
        return 0

    lax.fori_loop(0, 3, build, 0)

    loads[3].wait()
    collect(0, sums1)
    scale = 1.0 / jnp.sqrt(summed(sums1)[:, 0:1] + eps)
    has_env = jnp.where(seg > 0, 1.0, 0.0).astype(jnp.float32)
    has_x = jnp.where((sec > 0) & (sec < secs - 1), 1.0, 0.0).astype(jnp.float32)

    def scaled(i, held):
        return (held[chunk(i)].astype(jnp.float32) * scale).astype(jnp.bfloat16)

    def own(i, _):
        vec[chunk(i)] = scaled(i, start)
        return 0

    lax.fori_loop(0, CHUNKS, own, 0)

    right_z, right_x = right.at[1 - parity], right.at[parity]
    env_z, env_x = env.at[2 - parity], env.at[1 + parity]

    def first_z(i):
        z_copy(0, i).wait_recv()
        x_copy(i).start()
        piece = scaled(i, start_z)
        vec_z[chunk(i)] = piece
        low_z[chunk(i)] = dot(piece, right_z[...]).astype(jnp.bfloat16)

    def first_x(i):
        x_copy(i).wait_recv()
        low_x[chunk(i)] = (dot(scaled(i, start_x), right_x[...]) * has_x).astype(jnp.bfloat16)

    pairs = CHUNKS // 2

    def arrive(j, _):
        first_z(2 * j - 2)
        first_z(2 * j - 1)

        @pl.when(j > 1)
        def _():
            first_x(2 * j - 4)
            first_x(2 * j - 3)

        return 0

    def send_env(i, _):
        env_copy(i).start()
        return 0

    def arrive_send(j, _):
        send_env(2 * (j - ENV_AT), 0)
        send_env(2 * (j - ENV_AT) + 1, 0)
        return arrive(j, 0)

    lax.fori_loop(1, ENV_AT, arrive, 0)
    lax.fori_loop(ENV_AT, pairs, arrive_send, 0)
    lax.fori_loop(2 * (pairs - ENV_AT), CHUNKS, send_env, 0)
    first_z(CHUNKS - 2)
    first_z(CHUNKS - 1)
    for i in range(CHUNKS - 4, CHUNKS):
        first_x(i)

    def image_of(i):
        env_copy(i).wait_recv()
        value = dot(env[0, chunk(i)], vec[...])
        value += dot(env_z[chunk(i)], low_z[...])
        value += dot(env_x[chunk(i)], low_x[...])
        return jnp.where(mask(i * rows, rows), value * has_env, 0.0)

    def emit(i, value, guess, sums):
        mine = vec[chunk(i)].astype(jnp.float32)
        piece = value - guess * mine
        image[chunk(i)] = piece
        resid[chunk(i)] = piece.astype(jnp.bfloat16)
        z_copy(1, i).start()
        return sums[0] + total(mine * value), sums[1] + total(mine * mine)

    def quotient(along, size):
        return jnp.where(size > 0.0, along / jnp.where(size > 0.0, size, 1.0), 0.0)

    value = image_of(0)
    mine = vec[chunk(0)].astype(jnp.float32)
    guess = quotient(total(mine * value), total(mine * mine))
    sums = emit(0, value, guess, (zero, zero))

    def apply(i, sums):
        return emit(i, image_of(i), guess, sums)

    along, size = lax.fori_loop(1, CHUNKS, apply, sums)

    def turned(matrix, vector):
        for b in range(2):
            block = slice(b * half, (b + 1) * half)
            adj[block] = dot_left_t(matrix[:, block], vector[...]).astype(jnp.bfloat16)

    def pull_away(k, vector):
        turned(env_x, vector)

        def piece(b, _):
            pull_out[k, halves(b)] = (dot_right_t(adj[halves(b)], right_x[...]) * has_x).astype(jnp.bfloat16)
            return 0

        lax.fori_loop(0, 2, piece, 0)
        pull_copy(k).start()

    def pull_here(k, vector):
        turned(env_z, vector)

        def piece(b, _):
            pull[k, halves(b)] = dot_right_t(adj[halves(b)], right_z[...])
            return 0

        lax.fori_loop(0, 2, piece, 0)

    pull_away(0, resid)
    pull_away(1, vec)
    pull_here(0, resid)
    pull_here(1, vec)

    def diagonal(b, sums):
        image_r = dot(env[0, halves(b)], resid[...])
        image_v = dot(env[0, halves(b)], vec[...])
        mine_r, mine_v = resid[halves(b)].astype(jnp.float32), vec[halves(b)].astype(jnp.float32)
        return (
            sums[0] + total(mine_r * image_r),
            sums[1] + total(mine_r * image_v + mine_v * image_r),
            sums[2] + total(mine_v * image_v),
        )

    square_r, mixed, square_v = lax.fori_loop(0, 2, diagonal, (zero, zero, zero))
    ratio = quotient(along, size)

    def norms(i, sums):
        mine = vec[chunk(i)].astype(jnp.float32)
        piece = image[chunk(i)] + (guess - ratio) * mine
        return sums[0] + total(piece * piece), sums[1] + total(mine * piece)

    rho, cross = lax.fori_loop(0, CHUNKS, norms, (zero, zero))
    pull_copy(0).wait_recv()
    pull_copy(1).wait_recv()

    def join(i, sums):
        both = pull[0, chunk(i)] + pull_in[0, chunk(i)].astype(jnp.float32)
        pull[0, chunk(i)] = both
        base = vec_z[chunk(i)].astype(jnp.float32)
        return (
            sums[0] + total(both * base),
            sums[1] + total(pull[1, chunk(i)] * base),
            sums[2] + total(pull_in[1, chunk(i)].astype(jnp.float32) * base),
        )

    base_r, base_v, base_x = lax.fori_loop(0, CHUNKS, join, (zero, zero, zero))

    def meet(i, sums):
        z_copy(1, i).wait_recv()
        other = resid_z[chunk(i)].astype(jnp.float32)
        terms = (pull[0, chunk(i)], pull[1, chunk(i)], pull_in[1, chunk(i)].astype(jnp.float32))
        return tuple(old + jnp.sum(term * other, axis=0, keepdims=True) for old, term in zip(sums, terms))

    line_sums = lax.fori_loop(0, CHUNKS, meet, (jnp.zeros((1, width), jnp.float32),) * 3)
    met_r, met_v, met_x = [jnp.sum(line, axis=1, keepdims=True) for line in line_sums]
    sums2[pl.ds(sec, 1)] = pack(
        [along, size, rho, cross, ratio, guess]
        + [
            term * has_env
            for term in (square_r + met_r, mixed + met_v, square_v, met_x, base_r, base_v, base_x)
        ]
    )
    share(1, sums2)
    collect(1, sums2)

    gathered = sums2[...]
    column = lambda k: gathered[:, k : k + 1]
    over = lambda value: jnp.sum(value, axis=0, keepdims=True)
    alpha, size = over(column(0)), over(column(1))
    delta = column(4) - alpha
    resid_sq = jnp.maximum(over(column(2) + delta * (2.0 * column(3) + delta * column(1))), 0.0)
    overlap = over(column(3) + delta * column(1))
    beta_sq = resid_sq + eps
    beta = jnp.sqrt(beta_sq)
    inverse = 1.0 / beta
    own = column(5) - alpha
    deltas[...] = jnp.broadcast_to(own, deltas.shape)
    picked = lambda order: jnp.concatenate([deltas[s : s + 1] for s in order], axis=0)[:, 0:1]
    beside = picked([s + 1 - 2 * (s % 2) for s in range(secs)])
    across = picked([(s + 2 - 4 * (s % 2)) % secs for s in range(secs)])
    gamma = over(
        column(6) + own * (column(7) + own * column(8)) + across * column(9)
        + beside * (column(10) + own * column(11) + across * column(12))
    ) / beta_sq
    lowest = 0.5 * (alpha + gamma) - jnp.sqrt(0.25 * (alpha - gamma) ** 2 + beta_sq)
    first = gamma - lowest
    united_sq = first * first * size - 2.0 * first * overlap + resid_sq
    factor = math.sqrt(secs * width * width) / jnp.sqrt(jnp.maximum(united_sq, 0.0) + eps)
    back = deltas[pl.ds(sec, 1)][:, 0:1]

    def finish(i, _):
        mine = vec[chunk(i)].astype(jnp.float32)
        ritz = ((image[chunk(i)] + back * mine) * inverse).astype(jnp.bfloat16).astype(jnp.float32)
        ground[chunk(i)] = ((first * mine - beta * ritz) * factor).astype(jnp.bfloat16)
        return 0

    lax.fori_loop(0, CHUNKS, finish, 0)

    def drain(i, _):
        z_copy(0, i).wait_send()
        z_copy(1, i).wait_send()
        x_copy(i).wait_send()
        env_copy(i).wait_send()
        return 0

    lax.fori_loop(0, CHUNKS, drain, 0)
    pull_copy(0).wait_send()
    pull_copy(1).wait_send()

    rank = cols.shape[1]
    near = rank // 2
    low, high = slice(0, near), slice(near, rank)
    ground_back = back_copy(0, ground, ground_n)
    ground_back.start()
    loads[4].wait()
    kept_rank = table_ref[0, 2]
    keep = jnp.where(lax.broadcasted_iota(jnp.int32, (1, rank), 1) < kept_rank, 1.0, 0.0)
    row = lax.broadcasted_iota(jnp.int32, (rank, rank), 0)
    col = lax.broadcasted_iota(jnp.int32, (rank, rank), 1)
    gram[...] = jnp.where((row == col) & (col >= kept_rank), 1.0, 0.0)
    for b in range(2):
        block = slice(b * half, (b + 1) * half)
        ranged = (dot(ground[block], cols[...]) * keep).astype(jnp.bfloat16)
        turned_range = ranged.T
        range_t[:, block] = turned_range
        gram[...] += dot(turned_range, ranged)
    leading = invert_factor(gram[low, low], 8)
    basis_t[low] = split_dot(leading, range_t[low]).astype(jnp.bfloat16)
    backs = [back_copy(1 + b, basis_t.at[block], basis_n.at[block]) for b, block in enumerate((low, high))]
    backs[0].start()
    upper = fdot(leading, gram[low, high])
    upper_t = upper.T
    trailing = invert_factor(gram[high, high] - fdot(upper_t, upper), 8)
    corner = -fdot(trailing, fdot(upper_t, leading))
    basis_t[high] = (split_dot(corner, range_t[low]) + split_dot(trailing, range_t[high])).astype(jnp.bfloat16)
    backs[1].start()

    kept_ref[...] = rebuilt(basis_t[...], ground[...]).astype(jnp.bfloat16)

    ground_back.wait_recv()
    backs[0].wait_recv()
    part_n[...] = rebuilt(basis_n[low], ground_n[...])
    backs[1].wait_recv()
    next_ref[...] = (part_n[...] + rebuilt(basis_n[high], ground_n[...])).astype(jnp.bfloat16)
    ground_back.wait_send()
    for copy in backs:
        copy.wait_send()


def update(table, psi, site, terms, right, cols, secs):
    width = psi.shape[0]
    rank = cols.shape[1]
    square = (width, width)
    tall = pltpu.VMEM((rank, width), jnp.bfloat16)
    blocks = lambda *lead: pltpu.VMEM((*lead, *square), jnp.bfloat16)
    wide = pltpu.VMEM(square, jnp.float32)
    sums = pltpu.VMEM((secs, 128), jnp.float32)
    dma = pltpu.SemaphoreType.DMA
    return pl.pallas_call(
        update_kernel,
        out_shape=(jax.ShapeDtypeStruct(square, jnp.bfloat16),) * 2,
        in_specs=[pl.BlockSpec(memory_space=pltpu.SMEM)] + [pl.BlockSpec(memory_space=pl.ANY)] * 5,
        out_specs=(pl.BlockSpec(memory_space=pltpu.VMEM),) * 2,
        scratch_shapes=[
            blocks(), blocks(), blocks(3), blocks(2), pltpu.VMEM((width, rank), jnp.bfloat16),
            blocks(), blocks(), blocks(), blocks(), blocks(), blocks(3), blocks(3), blocks(), blocks(),
            blocks(), blocks(), wide, blocks(), blocks(), blocks(),
            pltpu.VMEM((2, *square), jnp.float32), blocks(2), blocks(2),
            sums, sums, pltpu.VMEM((secs, 128), jnp.float32),
            blocks(), blocks(), tall, tall, tall, pltpu.VMEM((rank, rank), jnp.float32), wide,
            dma((5,)), dma((2, CHUNKS)), dma((2, CHUNKS)), dma((CHUNKS,)), dma((CHUNKS,)),
            dma((CHUNKS,)), dma((CHUNKS,)), dma((2,)), dma((2,)), dma((2, secs)), dma((2, secs)), dma((3,)), dma((3,)),
        ],
        compiler_params=pltpu.CompilerParams(
            collective_id=1, has_side_effects=True, vmem_limit_bytes=62 * 2**20
        ),
        cost_estimate=pl.CostEstimate(flops=16 * 2 * width**3, bytes_accessed=8 * width**2, transcendentals=0),
    )(table, psi, site, terms, right, cols)


def finish_kernel(kept_ref, next_ref, out_ref, dens_ref):
    width = next_ref.shape[0]
    out_ref[...] = kept_ref[...]
    has_next = lax.axis_index("seg") < lax.axis_size("seg") - 1
    scale = jnp.where(has_next, 1.0 / width, 0.0).astype(jnp.float32)
    for b in range(2):
        block = slice(b * (width // 2), (b + 1) * (width // 2))
        dens_ref[block] = (dot_right_t(next_ref[block], next_ref[...]) * scale).astype(jnp.bfloat16)


def finish(kept, kept_next):
    square = jax.ShapeDtypeStruct(kept.shape, jnp.bfloat16)
    vmem = pl.BlockSpec(memory_space=pltpu.VMEM)
    return pl.pallas_call(
        finish_kernel,
        out_shape=(square, square),
        in_specs=[vmem, vmem],
        out_specs=(vmem, vmem),
        compiler_params=pltpu.CompilerParams(vmem_limit_bytes=62 * 2**20),
    )(kept, kept_next)


def per_device(psi_start, left_site, left_terms, right_terms, start_cols, sector_table):
    kept, kept_next = update(
        sector_table, psi_start[0, 0], left_site[0, 0], left_terms[0, 0], right_terms[0, 0],
        start_cols[0], lax.axis_size("sec"),
    )
    kept, back = finish(kept, kept_next)
    return (kept[None, None], back[None, None])


def solution(mesh):
    placed = (
        P("seg", "sec", None, None),
        P("seg", "sec", None, None),
        P("seg", "sec", None, None, None),
        P("seg", "sec", None, None, None),
        P("sec", None, None),
        P("sec", None),
    )
    return jax.shard_map(
        per_device,
        mesh=mesh,
        in_specs=placed,
        out_specs=(P("seg", "sec", None, None), P("seg", "sec", None, None)),
        check_vma=False,
    )
```
